32 devices in a mesh: ep: 8 (over y, x, core), dp: 4 (over z).
Axes of the slice: x: 2, y: 2, z: 4, core: 2. Of those that a mesh axis runs over, the one named last changes fastest.
Arguments:
- tokens: bfloat16 [8192, 1280], P(('ep', 'dp')), may hold values from -6 to 6
- expert_index: int32 [8192, 7], P(('ep', 'dp')), may hold values from 0 to 15, all different within a row; in each aligned block of 256 rows (0 to 255, 256 to 511, ...) at most 224 rows name the same one
- cotangent: bfloat16 [8192, 1280], P(('ep', 'dp')), may hold values from -6 to 6
- gains: float32 [1280, 2], P(('ep', 'dp')), may hold values from 0.5 to 1.5
- w_qkv: float32 [1280, 3840], P(('ep', 'dp')), may hold values from -0.15625 to 0.15625
- w_attn_out: float32 [1280, 1280], P(('ep', 'dp')), may hold values from -2.5 to 2.5
- w_router: float32 [1280, 16], P(('ep', 'dp')), may hold values from -0.078125 to 0.078125
- w_shared_in: float32 [1280, 1792], P(('ep', 'dp')), may hold values from -0.15625 to 0.15625
- w_shared_out: float32 [896, 1280], P(('ep', 'dp')), may hold values from -0.375 to 0.375
- w_expert_in: float32 [16, 1280, 1792], P('ep', 'dp'), may hold values from -0.15625 to 0.15625
- w_expert_out: float32 [16, 896, 1280], P('ep', 'dp'), may hold values from -2 to 2
Outputs:
- layer_out: bfloat16 [8192, 1280], P(('ep', 'dp'))
- tokens_grad: bfloat16 [8192, 1280], P(('ep', 'dp'))
- gains_grad: float32 [1280, 2], P(('ep', 'dp'))
- w_qkv_grad: float32 [1280, 3840], P(('ep', 'dp'))
- w_attn_out_grad: float32 [1280, 1280], P(('ep', 'dp'))
- w_router_grad: float32 [1280, 16], P(('ep', 'dp'))
- w_shared_in_grad: float32 [1280, 1792], P(('ep', 'dp'))
- w_shared_out_grad: float32 [896, 1280], P(('ep', 'dp'))
- w_expert_in_grad: float32 [16, 1280, 1792], P('ep', 'dp')
- w_expert_out_grad: float32 [16, 896, 1280], P('ep', 'dp')
The draws below stay inside these ranges and needn't reach their ends.
Inputs may be any that keep to these rules, and one draw needn't show every extreme that they name: `expert_index`: each token names 7 different experts. Among the 256 rows of one device (aligned blocks of rows) no expert is named more than 224 times, and in every draw some expert is named exactly 224 times by the rows of some device.
All inputs are finite; a program needn't handle non-finite values.
Results may differ from the reference program's by a relative error of at most 0.024.
Values may be sent and summed in bfloat16 or wider, within the bound.
No kernel may reach another device: no remote copies, remote signals or barrier semaphores. Data moves between devices by JAX's collectives and lax.ppermute only.
A program may use at most 320 MiB of HBM per device.

```python
import math
import jax
import jax.numpy as jnp
import numpy as np
from jax import lax

D = 1280
H = 10
DH = 128
EFF = 896
TOPK = 7
TOK_DEV = 256
EXPERTS = 16
SEQ = 1024
TOKENS = 8192
CAP = 224
N_EP = 8


def block_levels(own_key, shape, cuts, least, top_value):
    loudness = 1.0
    for position, parts in cuts:
        heights = jax.random.uniform(jax.random.fold_in(jax.random.fold_in(own_key, 6), position), (parts,), jnp.float32, least / len(cuts), top_value / len(cuts))
        loudness = loudness * jnp.repeat(jnp.exp(heights), shape[position] // parts).reshape((-1,) + (1,) * (len(shape) - 1 - position))
    return loudness


def deal_out(stream_key, own, number, rows, amount, top, bound, slope):
    sequence = jax.random.permutation(stream_key, amount)
    crowded, ordinary = portions_of(amount, rows * top, bound, slope, True), portions_of(amount, rows * top, bound, slope, False)
    places = jnp.arange(amount)

    def named(tallies, turn):
        used = int((tallies > 0).sum())
        fixed = max(1, used // 4)
        shifted = fixed + (places - fixed + turn * (used - fixed)) % max(1, amount - fixed)
        return jnp.zeros((amount,), jnp.int32).at[sequence[jnp.where(places < fixed, places, shifted)]].set(jnp.asarray(tallies, jnp.int32))

    tallies = jnp.where(number % 4 == 0, named(crowded, number // 4), named(ordinary, number - number // 4 - 1))
    mixed = jax.random.permutation(jax.random.fold_in(own, 3), amount)
    donor, taker = mixed[0:amount // 2 * 2:2], mixed[1:amount // 2 * 2:2]
    margin = jnp.minimum(tallies[donor] - 1, bound - tallies[taker]) // 2
    margin = jnp.where((donor == sequence[0]) | (taker == sequence[0]) | (tallies[taker] == 0), 0, jnp.maximum(margin, 0))
    shifted = jax.random.randint(jax.random.fold_in(own, 4), (amount // 2,), 0, 1 << 20) % (margin + 1)
    tallies = tallies.at[donor].add(-shifted).at[taker].add(shifted)
    labels = jnp.searchsorted(jnp.cumsum(tallies), jnp.arange(rows * top), side="right").astype(jnp.int32)
    table = labels.reshape(top, rows).T
    table = table[jax.random.permutation(jax.random.fold_in(own, 1), rows)]
    turn = jax.random.randint(jax.random.fold_in(own, 2), (rows, 1), 0, top)
    return jnp.take_along_axis(table, (jnp.arange(top)[None, :] + turn) % top, axis=1)


def portions_of(count, total, most, skew, full):
    loads = [(1 << 20) // math.isqrt(rank ** skew) + 1 for rank in range(1, count + 1)]
    largest = most if full else min(most, max(-(-total // count), total * loads[0] // sum(loads)))
    least = 1 if total - largest >= count - 1 else 0
    given, rest = [largest] + [least] * (count - 1), total - largest - least * (count - 1)
    while rest > 0:
        movable = [i for i in range(1, count) if given[i] < largest] or [i for i in range(1, count) if given[i] < most]
        whole, left = sum([loads[i] for i in movable]), rest
        for i in movable:
            addition = min(most - given[i], max(1, left * loads[i] // whole), rest)
            given[i] = given[i] + addition
            rest = rest - addition
    return np.array(given)


def noise(own_key, dims, spread, bound, cuts=(), kind=jnp.bfloat16):
    array = jax.random.normal(own_key, dims, jnp.float32) * spread
    if len(cuts) > 0:
        array = block_levels(own_key, dims, cuts, -0.22, 0.18) * array
    return jnp.clip(array, min=-bound, max=bound).astype(kind)


def setup_inputs(seed: int = 0) -> dict:
    arg_keys = jax.random.split(jax.random.key(seed), 12)
    tokens = noise(arg_keys[0], (TOKENS, D), 1.0, 6.0, ((0, 32),))
    expert_index_keys = jax.random.split(jax.random.fold_in(arg_keys[1], 1), TOKENS // TOK_DEV)
    expert_index_turns = jax.random.permutation(jax.random.fold_in(arg_keys[1], 3), TOKENS // TOK_DEV)
    expert_index = jax.vmap(lambda own, number: deal_out(jax.random.fold_in(arg_keys[1], 2), own, number, TOK_DEV, EXPERTS, TOPK, CAP, 2))(expert_index_keys, expert_index_turns).reshape((TOKENS, TOPK))
    cotangent = noise(arg_keys[2], (TOKENS, D), 1.0, 6.0, ((0, 32),))
    gains = jnp.clip(1.0 + 0.1 * jax.random.normal(arg_keys[3], (D, 2), jnp.float32), 0.5, 1.5)
    w_qkv = noise(arg_keys[4], (D, 3 * D), D ** -0.5, 0.15625, ((0, 32),), jnp.float32)
    w_attn_out = noise(arg_keys[5], (D, D), (max(D // 256, 1)) ** -0.5, 2.5, ((0, 32),), jnp.float32)
    w_router = noise(arg_keys[6], (D, EXPERTS), (4 * D) ** -0.5, 0.078125, ((0, 32),), jnp.float32)
    w_shared_in = noise(arg_keys[7], (D, 2 * EFF), D ** -0.5, 0.15625, ((0, 32),), jnp.float32)
    w_shared_out = noise(arg_keys[8], (EFF, D), (EFF // 3) ** -0.5, 0.375, ((0, 32),), jnp.float32)
    w_expert_in = noise(arg_keys[9], (EXPERTS, D, 2 * EFF), D ** -0.5, 0.15625, ((0, 8), (1, 4)), jnp.float32)
    w_expert_out = noise(arg_keys[10], (EXPERTS, EFF, D), (max(EFF // 112, 1)) ** -0.5, 2.0, ((0, 8), (1, 4)), jnp.float32)
    return dict(tokens=tokens, expert_index=expert_index, cotangent=cotangent, gains=gains, w_qkv=w_qkv, w_attn_out=w_attn_out, w_router=w_router, w_shared_in=w_shared_in, w_shared_out=w_shared_out, w_expert_in=w_expert_in, w_expert_out=w_expert_out)


EPS = 1e-06
HIGH = lax.Precision.HIGHEST

@jax.custom_vjp
def low(v):
    return lax.optimization_barrier(v.astype(jnp.bfloat16)).astype(jnp.float32)

@jax.custom_vjp
def low_back(v):
    return v

def low_keep(v):
    return (low(v), None)

def low_pass(kept, grad):
    return (grad,)

def back_keep(v):
    return (v, None)

def back_low(kept, grad):
    return (low(grad),)
low.defvjp(low_keep, low_pass)
low_back.defvjp(back_keep, back_low)

def rope_tables(positions):
    frequency = 10000.0 ** (-2.0 * jnp.arange(DH // 2, dtype=jnp.float32) / DH)
    angles = positions[:, None] * frequency[None, :]
    return (jnp.cos(angles)[:, None, :], jnp.sin(angles)[:, None, :])

def rotate(values, cosine_table, sine_table):
    half_size = values.shape[-1] // 2
    first_half = values[..., :half_size]
    second_half = values[..., half_size:]
    return jnp.concatenate([first_half * cosine_table - second_half * sine_table, first_half * sine_table + second_half * cosine_table], axis=-1)

def attend_block(queries, key_heads, values, first_row):
    scores = jnp.einsum('qhd,khd->qhk', queries, key_heads, precision=HIGH) * DH ** (-0.5)
    scores = low_back(scores)
    query_pos = first_row + jnp.arange(queries.shape[0], dtype=jnp.int32)
    key_pos = jnp.arange(key_heads.shape[0], dtype=jnp.int32)
    allowed = (key_pos[None, :] <= query_pos[:, None])[:, None, :]
    scores = jnp.where(allowed, scores, -1e+30)
    row_top = lax.optimization_barrier(jnp.max(scores, axis=-1, keepdims=True))
    weights = jnp.exp(scores - row_top)
    weights = weights / lax.optimization_barrier(jnp.sum(weights, axis=-1, keepdims=True))
    weights = low(weights)
    return jnp.einsum('qhk,khd->qhd', weights, values, precision=HIGH)
checked_block = jax.checkpoint(attend_block)

def attend_sequence(queries, key_heads, values):
    length = queries.shape[0]
    block_rows = min(512, length)
    block_count = length // block_rows
    starts = jnp.arange(block_count, dtype=jnp.int32) * block_rows
    pieces = queries.reshape(block_count, block_rows, H, DH)
    block_outs = lax.map(lambda block_item: checked_block(block_item[0], key_heads, values, block_item[1]), (pieces, starts))
    return block_outs.reshape(length, H, DH)

def swiglu(projected):
    return jax.nn.silu(projected[:, :EFF]) * projected[:, EFF:]

def expert_term(ffn_in, weight_in, weight_out, share_of):
    copies = low_back(ffn_in)
    projected = low_back(jnp.dot(copies, weight_in, precision=HIGH))
    inner_act = low(swiglu(projected))
    result = jnp.dot(inner_act, weight_out, precision=HIGH)
    result = low(low_back(result))
    return share_of[:, None] * result
checked_expert = jax.checkpoint(expert_term)

def reference(tokens, expert_index, cotangent, gains, w_qkv, w_attn_out, w_router, w_shared_in, w_shared_out, w_expert_in, w_expert_out):

    def forward(inputs, gains, w_qkv, w_attn_out, w_router, w_shared_in, w_shared_out, w_expert_in, w_expert_out):
        gains = low(gains)
        w_qkv = low(w_qkv)
        w_attn_out = low(w_attn_out)
        w_router = low(w_router)
        w_shared_in = low(w_shared_in)
        w_shared_out = low(w_shared_out)
        w_expert_in = low(w_expert_in)
        w_expert_out = low(w_expert_out)
        inv_first = lax.rsqrt(lax.optimization_barrier(jnp.mean(inputs * inputs, axis=-1, keepdims=True)) + EPS)
        attn_in = low(inputs * inv_first * gains[:, 0])
        projected = low_back(jnp.dot(attn_in, w_qkv, precision=HIGH))
        positions = jnp.arange(SEQ, dtype=jnp.int32).astype(jnp.float32)
        cosine_table, sine_table = rope_tables(positions)
        queries = low(rotate(projected[:, :D].reshape(N_EP, SEQ, H, DH), cosine_table, sine_table))
        key_heads = low(rotate(projected[:, D:2 * D].reshape(N_EP, SEQ, H, DH), cosine_table, sine_table))
        values = low(projected[:, 2 * D:].reshape(N_EP, SEQ, H, DH))
        attended = lax.map(lambda block_item: attend_sequence(block_item[0], block_item[1], block_item[2]), (queries, key_heads, values))
        attended = low(low_back(attended.reshape(TOKENS, D)))
        branch = low_back(jnp.dot(attended, w_attn_out, precision=HIGH))
        hidden = inputs + branch
        inv_second = lax.rsqrt(lax.optimization_barrier(jnp.mean(hidden * hidden, axis=-1, keepdims=True)) + EPS)
        ffn_in = low(hidden * inv_second * gains[:, 1])
        logits = low_back(jnp.dot(ffn_in, w_router, precision=HIGH))
        router_probs = jax.nn.softmax(logits, axis=-1)
        gate_values = jnp.take_along_axis(router_probs, expert_index, axis=1)
        shared_pre = low_back(jnp.dot(ffn_in, w_shared_in, precision=HIGH))
        shared_act = low(swiglu(shared_pre))
        shared_out = low_back(jnp.dot(shared_act, w_shared_out, precision=HIGH))

        def add_expert(running, block_item):
            weight_in, weight_out, number = block_item
            share_of = lax.optimization_barrier(jnp.sum(jnp.where(expert_index == number, gate_values, 0.0), axis=1))
            return (running + checked_expert(ffn_in, weight_in, weight_out, share_of), None)
        routed, _ = lax.scan(add_expert, jnp.zeros((TOKENS, D), jnp.float32), (w_expert_in, w_expert_out, jnp.arange(EXPERTS, dtype=jnp.int32)))
        return hidden + shared_out + routed
    layer_value, pull = jax.vjp(forward, tokens.astype(jnp.float32), gains, w_qkv, w_attn_out, w_router, w_shared_in, w_shared_out, w_expert_in, w_expert_out)
    grads = pull(cotangent.astype(jnp.float32))
    return (layer_value.astype(jnp.bfloat16), grads[0].astype(jnp.bfloat16), grads[1], grads[2], grads[3], grads[4], grads[5], grads[6], grads[7], grads[8])
```

```python
import functools

import jax
import jax.numpy as jnp
from jax import lax
from jax.experimental import pallas as pl
from jax.experimental.pallas import tpu as pltpu
from jax.sharding import PartitionSpec as P

H = 10
DH = 128
EFF = 896
EPS = 1e-06
NEG = -1e30
FAR = 1 << 30

bf16 = jnp.bfloat16
f32 = jnp.float32


def contract_rows(left_side, right_side):
    return lax.dot_general(
        left_side, right_side, (((0,), (0,)), ((), ())), preferred_element_type=f32
    )


def times_transposed(left_side, right_side):
    return lax.dot_general(
        left_side, right_side, (((1,), (1,)), ((), ())), preferred_element_type=f32
    )


def matmul(left_side, right_side):
    return jnp.dot(left_side, right_side, preferred_element_type=f32)


def swiglu_back(gate_part, up_part, act_grad):
    sigma_gate = jax.nn.sigmoid(gate_part)
    silu_gate = gate_part * sigma_gate
    slope = sigma_gate * (1.0 + gate_part * (1.0 - sigma_gate))
    return jnp.concatenate([act_grad * up_part * slope, act_grad * silu_gate], axis=-1)


def flip(x, bit):
    count = lax.axis_size("ep")
    return lax.ppermute(x, "ep", [(i, i ^ bit) for i in range(count)])


def turn(x, step):
    count = lax.axis_size("dp")
    return lax.ppermute(x, "dp", [(i, (i + step) % count) for i in range(count)])


def earlier_blocks(x):
    count = lax.axis_size("dp")
    blocks = [x]
    for hop in range(1, count):
        blocks.append(lax.ppermute(blocks[-1], "dp", [(i, i + 1) for i in range(hop - 1, count - 1)]))
    return blocks


def sum_to_owner(parts):
    count = lax.axis_size("dp")
    total = parts[count - 1]
    for k in range(count - 1, 0, -1):
        arrived = lax.ppermute(total.astype(bf16), "dp", [(i, i - 1) for i in range(k, count)])
        total = parts[k - 1] + arrived.astype(f32)
    return total


def gather_ep(x):
    half = x.shape[0] // 2
    core = flip(x, 1)
    side = flip(x, 2)
    down = flip(x, 4)
    far = [flip(down[:half], 2), flip(side[half:], 4)]
    side_core = flip(side, 1)
    down_core = flip(down, 1)
    far_core = [flip(far[0], 1), flip(far[1], 1)]
    return [[x], [core], [side], [side_core], [down], [down_core], far, far_core]


def scatter_ep(kept, sent):
    add = lambda a, b: a.astype(f32) + b.astype(f32)
    mine = add(kept, flip(sent, 1)).astype(bf16)
    half = mine.shape[1] // 2
    left, right = mine[:, :half], mine[:, half:]
    left_two = add(left[0::2], flip(left[1::2], 2)).astype(bf16)
    right_two = add(right[:2], flip(right[2:], 4)).astype(bf16)
    left_one = add(left_two[0], flip(left_two[1], 4))
    right_one = add(right_two[0], flip(right_two[1], 2))
    return jnp.concatenate([left_one, right_one], axis=0)


def gather_dp(x):
    count = lax.axis_size("dp")
    if count != 4:
        return lax.all_gather(x, "dp", axis=0, tiled=False)
    place = lax.axis_index("dp")
    width = x.shape[-1]
    half = (width // 256) * 128
    behind = turn(x, 1)
    ahead = turn(x, -1)
    across = jnp.concatenate([turn(behind[..., :half], 1), turn(ahead[..., half:], -1)], axis=-1)
    whole = jnp.zeros((count,) + x.shape, x.dtype)
    for step, block in ((0, x), (1, behind), (2, across), (3, ahead)):
        whole = lax.dynamic_update_slice(
            whole, block[None], (lax.rem(place - step + count, count),) + (0,) * x.ndim
        )
    return whole


def gather_rows(x):
    rows, width = x.shape
    here = lax.axis_index("ep")
    line = gather_dp(x)
    places = line.shape[0]
    blocks = gather_ep(line)
    whole = jnp.zeros((len(blocks), places, rows, width), x.dtype)
    for k, pieces in enumerate(blocks):
        start = 0
        for piece in pieces:
            whole = lax.dynamic_update_slice(whole, piece[None], (here ^ k, start, 0, 0))
            start += piece.shape[0]
    return whole.reshape(len(blocks) * places * rows, width)


def pick(x, index, axis):
    return lax.dynamic_index_in_dim(x, index, axis, keepdims=False)


def scatter_rows(x):
    ways, places = lax.axis_size("ep"), lax.axis_size("dp")
    rows, width = x.shape[0] // (ways * places), x.shape[1]
    here, place = lax.axis_index("ep"), lax.axis_index("dp")
    core, side, down = here & 1, (here >> 1) & 1, (here >> 2) & 1
    add = lambda a, b: a.astype(f32) + b.astype(f32)
    blocks = x.astype(bf16).reshape(2, 2, 2, places, rows, width)
    one = add(pick(blocks, core, 2), flip(pick(blocks, 1 - core, 2), 1)).astype(bf16)
    half = places // 2
    left, right = one[:, :, :half], one[:, :, half:]
    left = add(pick(left, side, 1), flip(pick(left, 1 - side, 1), 2)).astype(bf16)
    right = add(pick(right, down, 0), flip(pick(right, 1 - down, 0), 4)).astype(bf16)
    left = add(pick(left, down, 0), flip(pick(left, 1 - down, 0), 4)).astype(bf16)
    right = add(pick(right, side, 0), flip(pick(right, 1 - side, 0), 2)).astype(bf16)
    line = jnp.concatenate([left, right], axis=0)
    if places != 4:
        return lax.psum_scatter(
            line.reshape(places * rows, width), "dp", scatter_dimension=0, tiled=True
        ).astype(f32)
    cut = (width // 256) * 128
    at = lambda step: pick(line, lax.rem(place + step, places), 0)
    across = at(2)
    first = turn(across[:, :cut], 1)
    second = turn(across[:, cut:], -1)
    ahead, behind = at(1), at(3)
    ahead = jnp.concatenate([add(ahead[:, :cut], first).astype(bf16), ahead[:, cut:]], axis=1)
    behind = jnp.concatenate([behind[:, :cut], add(behind[:, cut:], second).astype(bf16)], axis=1)
    return at(0).astype(f32) + add(turn(ahead, 1), turn(behind, -1))


def spin(x, cosine, sine):
    return x * cosine + pltpu.roll(x, DH // 2, 1) * sine


def unspin(x, cosine, sine):
    return x * cosine - pltpu.roll(x, DH // 2, 1) * sine


def attend_kernel(
    x_ref, wq_ref, wk_ref, wv_ref, cos_ref, sin_ref, kpos_ref, qpos_ref, o_ref, q_ref, k_ref, v_ref
):
    rows = o_ref.shape[0]
    scale = DH ** (-0.5)
    keys = matmul(x_ref[...], wk_ref[...])
    values = matmul(x_ref[...], wv_ref[...]).astype(bf16)
    queries = matmul(x_ref[:rows], wq_ref[...])
    v_ref[...] = values
    allowed = kpos_ref[...] <= qpos_ref[...]
    for head in range(keys.shape[1] // DH):
        part = slice(head * DH, (head + 1) * DH)
        k = spin(keys[:, part], cos_ref[...], sin_ref[...]).astype(bf16)
        q = spin(queries[:, part], cos_ref[:rows], sin_ref[:rows]).astype(bf16)
        k_ref[:, part] = k
        q_ref[:, part] = q
        scores = jnp.where(allowed, times_transposed(q, k) * scale, NEG)
        top = jnp.max(scores, axis=1, keepdims=True)
        weights = jnp.exp(scores - top)
        total = jnp.sum(weights, axis=1, keepdims=True)
        attended = matmul(weights.astype(bf16), values[:, part]) / total
        o_ref[:, part] = attended.astype(bf16)


def attend(x, wq, wk, wv, cosine, sine, kpos, qpos, rows):
    length, width = x.shape
    cols = 2 * DH
    once = pl.Buffered(1)
    fixed = lambda a: pl.BlockSpec(a.shape, lambda h: (0, 0), pipeline_mode=once)
    wide = lambda r: pl.BlockSpec((r, cols), lambda h: (0, h))
    shape = lambda r: jax.ShapeDtypeStruct((r, H * DH), bf16)
    return pl.pallas_call(
        attend_kernel,
        grid=(H * DH // cols,),
        in_specs=[fixed(x), wide(width), wide(width), wide(width)]
        + [fixed(cosine), fixed(sine), fixed(kpos), fixed(qpos)],
        out_specs=[wide(rows), wide(rows), wide(length), wide(length)],
        out_shape=[shape(rows), shape(rows), shape(length), shape(length)],
        compiler_params=pltpu.CompilerParams(vmem_limit_bytes=56 << 20),
        cost_estimate=pl.CostEstimate(
            flops=2 * width * H * DH * (2 * length + rows) + 4 * rows * length * H * DH,
            bytes_accessed=2 * (3 * width * H * DH + 3 * length * width),
            transcendentals=rows * length * H,
        ),
    )(x, wq, wk, wv, cosine, sine, kpos, qpos)


def attend_back_kernel(
    q_ref, k_ref, v_ref, do_ref, cos_ref, sin_ref, kpos_ref, qpos_ref, dq_ref, dk_ref, dv_ref
):
    rows = q_ref.shape[0]
    scale = DH ** (-0.5)
    allowed = kpos_ref[...] <= qpos_ref[...]
    q, k, v, do = q_ref[...], k_ref[...], v_ref[...], do_ref[...]
    scores = jnp.where(allowed, times_transposed(k, q) * scale, NEG)
    top = jnp.max(scores, axis=0, keepdims=True)
    weights = jnp.exp(scores - top)
    weights = weights * (1.0 / jnp.sum(weights, axis=0, keepdims=True))
    weight_grad = times_transposed(v, do)
    delta = jnp.sum(weights * weight_grad, axis=0, keepdims=True)
    score_grad = (weights * (weight_grad - delta)).astype(bf16)
    dv_ref[...] = matmul(weights.astype(bf16), do).astype(bf16)
    dk = matmul(score_grad, q) * scale
    dk_ref[...] = unspin(dk, cos_ref[...], sin_ref[...]).astype(bf16)
    dq = contract_rows(score_grad, k) * scale
    dq_ref[...] = unspin(dq, cos_ref[:rows], sin_ref[:rows]).astype(bf16)


def attend_back(q, k, v, do, cosine, sine, kpos, qpos):
    rows, length = q.shape[0], k.shape[0]
    once = pl.Buffered(1)
    fixed = lambda a: pl.BlockSpec(a.shape, lambda h: (0, 0), pipeline_mode=once)
    wide = lambda r: pl.BlockSpec((r, DH), lambda h: (0, h))
    shape = lambda r: jax.ShapeDtypeStruct((r, H * DH), bf16)
    return pl.pallas_call(
        attend_back_kernel,
        grid=(H,),
        in_specs=[wide(rows), wide(length), wide(length), wide(rows)]
        + [fixed(cosine), fixed(sine), fixed(kpos), fixed(qpos)],
        out_specs=[wide(rows), wide(length), wide(length)],
        out_shape=[shape(rows), shape(length), shape(length)],
        compiler_params=pltpu.CompilerParams(vmem_limit_bytes=56 << 20),
        cost_estimate=pl.CostEstimate(
            flops=10 * rows * length * H * DH,
            bytes_accessed=2 * 4 * length * H * DH,
            transcendentals=rows * length * H,
        ),
    )(q, k, v, do, cosine, sine, kpos, qpos)


def per_device(
    tokens,
    expert_index,
    cotangent,
    gains,
    w_qkv,
    w_attn_out,
    w_router,
    w_shared_in,
    w_shared_out,
    w_expert_in,
    w_expert_out,
):
    rows, width = tokens.shape
    ways, places = lax.axis_size("ep"), lax.axis_size("dp")
    here, place = lax.axis_index("ep"), lax.axis_index("dp")
    local = w_expert_in.shape[0]
    experts = local * ways

    token_blocks = earlier_blocks(tokens)
    small = jnp.concatenate(
        [w_router.astype(bf16), gains.astype(bf16), jnp.zeros((gains.shape[0], 128 - experts - 2), bf16)],
        axis=1,
    )
    small = gather_rows(small)
    qkv_low = w_qkv.astype(bf16)
    wk = gather_rows(qkv_low[:, width : 2 * width])
    wv = gather_rows(qkv_low[:, 2 * width :])
    wq = gather_rows(qkv_low[:, :width])
    attn_weight = gather_rows(w_attn_out.astype(bf16))
    shared_in_weight = gather_rows(w_shared_in.astype(bf16))
    shared_out_weight = gather_rows(w_shared_out.astype(bf16))
    expert_in_low, expert_out_low = w_expert_in.astype(bf16), w_expert_out.astype(bf16)
    expert_in_weight, expert_out_weight = [], []
    for e in range(local):
        expert_in_weight.append(lax.all_gather(expert_in_low[e], "dp", axis=0, tiled=True))
        expert_out_weight.append(lax.all_gather(expert_out_low[e], "dp", axis=0, tiled=True))
    choose = jnp.sum(
        (expert_index[:, :, None] == jnp.arange(experts, dtype=jnp.int32)).astype(f32), axis=1
    )
    order = (0, 2, 4, 6, 1, 3, 5, 7)

    def lay(blocks):
        return jnp.concatenate([piece for k in order for piece in blocks[k]], axis=0)

    upstream_all = lay(gather_ep(cotangent))
    choose_all = lay(gather_ep(choose.astype(bf16)))

    router_weight = small[:, :experts]
    gain_attn = small[:, experts].astype(f32)
    gain_ffn = small[:, experts + 1].astype(f32)

    inputs_all = jnp.concatenate(token_blocks, axis=0).astype(f32)
    inv_first = lax.rsqrt(jnp.mean(inputs_all * inputs_all, axis=-1, keepdims=True) + EPS)
    normed_first = inputs_all * inv_first
    attn_in = (normed_first * gain_attn).astype(bf16)
    inputs = tokens.astype(f32)
    lane = jnp.arange(rows, dtype=jnp.int32)
    steps = jnp.arange(places, dtype=jnp.int32)
    positions = ((place - steps)[:, None] * rows + lane[None, :]).reshape(-1)
    key_pos = jnp.where(positions >= 0, positions, FAR)
    query_pos = place * rows + lane
    frequency = 10000.0 ** (-2.0 * jnp.arange(DH // 2, dtype=f32) / DH)
    angles = positions.astype(f32)[:, None] * frequency[None, :]
    cosine, sine = jnp.cos(angles), jnp.sin(angles)
    cosine = jnp.concatenate([cosine, cosine], axis=1)
    sine = jnp.concatenate([-sine, sine], axis=1)
    attended_low, queries, keys, values = attend(
        attn_in, wq, wk, wv, cosine, sine, key_pos[None, :], query_pos[:, None], rows
    )
    hidden = inputs + matmul(attended_low, attn_weight)
    inv_second = lax.rsqrt(jnp.mean(hidden * hidden, axis=-1, keepdims=True) + EPS)
    normed_second = hidden * inv_second
    ffn_in = (normed_second * gain_ffn).astype(bf16)

    ffn_all = lay(gather_ep(ffn_in))

    def route(rows_in):
        logits = matmul(rows_in, router_weight)
        raised = jnp.exp(logits - jnp.max(logits, axis=-1, keepdims=True))
        return raised / jnp.sum(raised, axis=-1, keepdims=True)

    router_probs = route(ffn_in)

    shared_pre = matmul(ffn_in, shared_in_weight)
    shared_gate, shared_up = shared_pre[:, :EFF], shared_pre[:, EFF:]
    shared_act = (jax.nn.silu(shared_gate) * shared_up).astype(bf16)
    shared_out = matmul(shared_act, shared_out_weight)
    shared_act_grad = times_transposed(cotangent, shared_out_weight)
    shared_pre_grad = swiglu_back(shared_gate, shared_up, shared_act_grad).astype(bf16)
    shared_out_part = scatter_rows(contract_rows(shared_act, cotangent).astype(bf16))
    shared_in_part = scatter_rows(contract_rows(ffn_in, shared_pre_grad).astype(bf16))
    shared_back = times_transposed(shared_pre_grad, shared_in_weight)

    gates_all = route(ffn_all) * choose_all.astype(f32)
    upstream_wide = upstream_all.astype(f32)
    expert_ids = jnp.arange(experts, dtype=jnp.int32)
    routed = 0.0
    back = 0.0
    gate_grads, in_parts, out_parts = [], [], []
    for e in range(local):
        gate = jnp.sum(jnp.where(expert_ids == here * local + e, gates_all, 0.0), axis=1, keepdims=True)
        pre = matmul(ffn_all, expert_in_weight[e])
        pre_gate, pre_up = pre[:, :EFF], pre[:, EFF:]
        act = (jax.nn.silu(pre_gate) * pre_up).astype(bf16)
        result = matmul(act, expert_out_weight[e]).astype(bf16).astype(f32)
        routed = routed + gate * result
        gate_grads.append(jnp.sum(upstream_wide * result, axis=-1))
        copy_grad = (gate * upstream_wide).astype(bf16)
        act_grad = times_transposed(copy_grad, expert_out_weight[e])
        pre_grad = swiglu_back(pre_gate, pre_up, act_grad).astype(bf16)
        out_parts.append(
            lax.psum_scatter(
                contract_rows(act, copy_grad).astype(bf16), "dp", scatter_dimension=0, tiled=True
            ).astype(f32)
        )
        in_parts.append(
            lax.psum_scatter(
                contract_rows(ffn_all, pre_grad).astype(bf16), "dp", scatter_dimension=0, tiled=True
            ).astype(f32)
        )
        back = back + times_transposed(pre_grad, expert_in_weight[e])
    expert_in_part = jnp.stack(in_parts, axis=0)
    expert_out_part = jnp.stack(out_parts, axis=0)

    def home(total):
        total = total.astype(bf16)
        return scatter_ep(
            total[: ways // 2 * rows].reshape(ways // 2, rows, -1),
            total[ways // 2 * rows :].reshape(ways // 2, rows, -1),
        )

    routed_in_grad = home(back)
    layer_out = (hidden + shared_out + home(routed)).astype(bf16)

    gate_grads = jnp.stack(gate_grads, axis=0).reshape(local, ways, rows)
    prob_grad = 0.0
    for slot, k in enumerate(order):
        piece = gate_grads[:, slot]
        if k:
            piece = flip(piece, k)
        for e in range(local):
            prob_grad = prob_grad + jnp.where(
                expert_ids == (here ^ k) * local + e, piece[e][:, None], 0.0
            )
    prob_grad = prob_grad * choose
    logit_grad = (
        router_probs * (prob_grad - jnp.sum(router_probs * prob_grad, axis=-1, keepdims=True))
    ).astype(bf16)
    router_grad = contract_rows(ffn_in, logit_grad)

    upstream = cotangent.astype(f32)
    ffn_in_grad = routed_in_grad + times_transposed(logit_grad, router_weight) + shared_back
    gain_ffn_grad = jnp.sum(ffn_in_grad * normed_second, axis=0)
    scaled_second = ffn_in_grad * gain_ffn
    hidden_grad = upstream + inv_second * (
        scaled_second
        - normed_second * jnp.mean(scaled_second * normed_second, axis=-1, keepdims=True)
    )
    branch_grad = hidden_grad.astype(bf16)
    attended_grad = times_transposed(branch_grad, attn_weight).astype(bf16)
    attn_out_part = scatter_rows(contract_rows(attended_low, branch_grad).astype(bf16))

    query_grad, key_grad, value_grad = attend_back(
        queries, keys, values, attended_grad, cosine, sine, key_pos[:, None], query_pos[None, :]
    )
    query_part = scatter_rows(contract_rows(attn_in[:rows], query_grad).astype(bf16))
    key_part = scatter_rows(contract_rows(attn_in, key_grad).astype(bf16))
    value_part = scatter_rows(contract_rows(attn_in, value_grad).astype(bf16))
    attn_in_grads = times_transposed(key_grad, wk) + times_transposed(value_grad, wv)
    query_back = times_transposed(query_grad, wq)
    first = attn_in_grads[:rows] + query_back
    gain_attn_grad = jnp.sum(attn_in_grads * normed_first, axis=0) + jnp.sum(
        query_back * normed_first[:rows], axis=0
    )
    attn_in_grad = sum_to_owner(
        [first] + [attn_in_grads[k * rows : (k + 1) * rows] for k in range(1, places)]
    )
    small_grad = jnp.concatenate(
        [
            router_grad,
            gain_attn_grad[:, None],
            gain_ffn_grad[:, None],
            jnp.zeros((width, 256 - experts - 2), f32),
        ],
        axis=1,
    )
    small_part = scatter_rows(small_grad.astype(bf16))
    normed_own, inv_own = normed_first[:rows], inv_first[:rows]
    scaled_first = attn_in_grad * gain_attn
    input_grad = hidden_grad + inv_own * (
        scaled_first - normed_own * jnp.mean(scaled_first * normed_own, axis=-1, keepdims=True)
    )
    return (
        layer_out,
        input_grad.astype(bf16),
        small_part[:, experts : experts + 2],
        jnp.concatenate([query_part, key_part, value_part], axis=1),
        attn_out_part,
        small_part[:, :experts],
        shared_in_part,
        shared_out_part,
        expert_in_part,
        expert_out_part,
    )


def solution(mesh):
    both = P(("ep", "dp"), None)
    cut = P("ep", "dp", None)
    return jax.shard_map(
        per_device,
        mesh=mesh,
        in_specs=(both,) * 9 + (cut,) * 2,
        out_specs=(both,) * 8 + (cut,) * 2,
        check_vma=False,
    )
```

```python
import functools

import jax
import jax.numpy as jnp
from jax import lax
from jax.experimental import pallas as pl
from jax.experimental.pallas import tpu as pltpu
from jax.sharding import PartitionSpec as P

H = 10
DH = 128
EFF = 896
EPS = 1e-06
NEG = -1e30
FAR = 1 << 30

bf16 = jnp.bfloat16
f32 = jnp.float32


def contract_rows(left_side, right_side):
    return lax.dot_general(
        left_side, right_side, (((0,), (0,)), ((), ())), preferred_element_type=f32
    )


def times_transposed(left_side, right_side):
    return lax.dot_general(
        left_side, right_side, (((1,), (1,)), ((), ())), preferred_element_type=f32
    )


def matmul(left_side, right_side):
    return jnp.dot(left_side, right_side, preferred_element_type=f32)


def swiglu_back(gate_part, up_part, act_grad):
    sigma_gate = jax.nn.sigmoid(gate_part)
    silu_gate = gate_part * sigma_gate
    slope = sigma_gate * (1.0 + gate_part * (1.0 - sigma_gate))
    return jnp.concatenate([act_grad * up_part * slope, act_grad * silu_gate], axis=-1)


def flip(x, bit):
    count = lax.axis_size("ep")
    return lax.ppermute(x, "ep", [(i, i ^ bit) for i in range(count)])


def flip_dp(x, bit):
    count = lax.axis_size("dp")
    return lax.ppermute(x, "dp", [(i, i ^ bit) for i in range(count)])


def add(a, b):
    return a.astype(f32) + b.astype(f32)


def after(*values):
    there = iter(lax.optimization_barrier(tuple(v for v in values if v is not None)))
    return tuple(None if v is None else next(there) for v in values)


def pick(x, index, axis):
    return lax.dynamic_index_in_dim(x, index, axis, keepdims=False)


def put(whole, part, index):
    return lax.dynamic_update_slice(whole, part, (index,) + (0,) * (whole.ndim - 1))


def earlier_blocks(x):
    count = lax.axis_size("dp")
    return [x] + [
        lax.ppermute(x, "dp", [(i, i + step) for i in range(count - step)]) for step in range(1, count)
    ]


def place_bits():
    here, place = lax.axis_index("ep"), lax.axis_index("dp")
    return here & 1, (here >> 1) & 1, (here >> 2) & 1, place & 1, place >> 1


def spread_near(x):
    return [flip(x, 2), flip(x, 4)]


def spread_far(side, down):
    half = side.shape[0] // 2
    return flip(down[:half], 2), flip(side[half:], 4)


def spread_chips(x, side, down, far):
    chip = lax.axis_index("ep") >> 1
    mine = jnp.zeros((4,) + x.shape, x.dtype)
    for k, block in enumerate((x, side, down, jnp.concatenate(far, axis=0))):
        mine = put(mine, block[None], chip ^ k)
    return mine


def line_near(x):
    if lax.axis_size("dp") != 4:
        return [lax.all_gather(x, "dp", axis=0, tiled=False)]
    return [flip_dp(x, bit) for bit in (1, 2, 3)]


def line_end(x, blocks):
    if len(blocks) == 1:
        return blocks[0]
    place = lax.axis_index("dp")
    whole = jnp.zeros((4,) + x.shape, x.dtype)
    for k, block in enumerate([x] + blocks):
        whole = put(whole, block[None], place ^ k)
    return whole


def rows_whole(mine):
    other = flip(mine, 1)
    core = lax.axis_index("ep") & 1
    both = jnp.zeros((4, 2) + mine.shape[1:], mine.dtype)
    both = lax.dynamic_update_slice(both, mine[:, None], (0, core, 0, 0, 0))
    both = lax.dynamic_update_slice(both, other[:, None], (0, 1 - core, 0, 0, 0))
    return both.reshape(-1, mine.shape[-1])


def split_near(one):
    _, side, down, _, _ = place_bits()
    left, right = one[:, :, 0], one[:, :, 1]
    return [
        pick(left, side, 1),
        pick(right, down, 0),
        flip(pick(left, 1 - side, 1), 2),
        flip(pick(right, 1 - down, 0), 4),
    ]


def split_far(left, right, from_side, from_down):
    _, side, down, _, _ = place_bits()
    left = add(left, from_side).astype(bf16)
    right = add(right, from_down).astype(bf16)
    return [
        pick(left, down, 0),
        pick(right, side, 0),
        flip(pick(left, 1 - down, 0), 4),
        flip(pick(right, 1 - side, 0), 2),
    ]


def collect_near(mine, arrived):
    one = add(mine, arrived).astype(bf16)
    return split_near(one.reshape(2, 2, 2, one.shape[1] // 2, one.shape[2]))


def collect_end(left, right, from_down, from_side):
    return jnp.concatenate([add(left, from_down), add(right, from_side)], axis=0)


def rows_core(parts):
    ways, places = lax.axis_size("ep"), lax.axis_size("dp")
    core, _, _, _, _ = place_bits()
    blocks = [
        x.reshape(2, 2, 2, places, x.shape[0] // (ways * places), x.shape[1]) for x in parts
    ]
    half = lambda which: jnp.concatenate([pick(x, which, 2) for x in blocks], axis=-1)
    return half(core), flip(half(1 - core), 1)


def rows_near(kept, arrived):
    one = add(kept, arrived).astype(bf16)
    places = one.shape[2]
    return split_near(one.reshape(one.shape[:2] + (2, places // 2) + one.shape[3:]))


def rows_line(left, right, from_down, from_side):
    left = add(left, from_down).astype(bf16)
    right = add(right, from_side).astype(bf16)
    line = jnp.concatenate([left, right], axis=0)
    _, _, _, odd, _ = place_bits()
    if line.shape[0] != 4:
        rows, width = line.shape[1:]
        total = lax.psum_scatter(
            line.reshape(-1, width), "dp", scatter_dimension=0, tiled=True
        )
        return total, total
    line = line.reshape((2, 2) + line.shape[1:])
    return pick(line, odd, 1), flip_dp(pick(line, 1 - odd, 1), 1)


def rows_last(kept, arrived):
    if kept.ndim == 2:
        return kept.astype(f32), None
    _, _, _, _, upper = place_bits()
    line = add(kept, arrived).astype(bf16)
    return pick(line, upper, 0), flip_dp(pick(line, 1 - upper, 0), 2)


def rows_end(kept, arrived):
    return kept if arrived is None else add(kept, arrived)


def spin(x, cosine, sine):
    return x * cosine + pltpu.roll(x, DH // 2, 1) * sine


def unspin(x, cosine, sine):
    return x * cosine - pltpu.roll(x, DH // 2, 1) * sine


def attend_kernel(
    x_ref, wq_ref, wk_ref, wv_ref, cos_ref, sin_ref, kpos_ref, qpos_ref, o_ref, q_ref, k_ref, v_ref
):
    rows = o_ref.shape[0]
    scale = DH ** (-0.5)
    keys = matmul(x_ref[...], wk_ref[...])
    values = matmul(x_ref[...], wv_ref[...]).astype(bf16)
    queries = matmul(x_ref[:rows], wq_ref[...])
    v_ref[...] = values
    allowed = kpos_ref[...] <= qpos_ref[...]
    for head in range(keys.shape[1] // DH):
        part = slice(head * DH, (head + 1) * DH)
        k = spin(keys[:, part], cos_ref[...], sin_ref[...]).astype(bf16)
        q = spin(queries[:, part], cos_ref[:rows], sin_ref[:rows]).astype(bf16)
        k_ref[:, part] = k
        q_ref[:, part] = q
        scores = jnp.where(allowed, times_transposed(q, k) * scale, NEG)
        top = jnp.max(scores, axis=1, keepdims=True)
        weights = jnp.exp(scores - top)
        total = jnp.sum(weights, axis=1, keepdims=True)
        attended = matmul(weights.astype(bf16), values[:, part]) / total
        o_ref[:, part] = attended.astype(bf16)


def attend(x, weights, cosine, sine, kpos, qpos, rows):
    length, width = x.shape
    cols = 2 * DH
    once = pl.Buffered(1)
    fixed = lambda a: pl.BlockSpec(a.shape, lambda h: (0, 0), pipeline_mode=once)
    wide = lambda r: pl.BlockSpec((r, cols), lambda h: (0, h))
    steps = H * DH // cols
    part = lambda n: pl.BlockSpec((width, cols), lambda h, n=n: (0, h + n * steps))
    shape = lambda r: jax.ShapeDtypeStruct((r, H * DH), bf16)
    return pl.pallas_call(
        attend_kernel,
        grid=(steps,),
        in_specs=[fixed(x), part(0), part(1), part(2)]
        + [fixed(cosine), fixed(sine), fixed(kpos), fixed(qpos)],
        out_specs=[wide(rows), wide(rows), wide(length), wide(length)],
        out_shape=[shape(rows), shape(rows), shape(length), shape(length)],
        compiler_params=pltpu.CompilerParams(vmem_limit_bytes=56 << 20),
        cost_estimate=pl.CostEstimate(
            flops=2 * width * H * DH * (2 * length + rows) + 4 * rows * length * H * DH,
            bytes_accessed=2 * (3 * width * H * DH + 3 * length * width),
            transcendentals=rows * length * H,
        ),
    )(x, weights, weights, weights, cosine, sine, kpos, qpos)


def attend_back_kernel(
    q_ref, k_ref, v_ref, do_ref, cos_ref, sin_ref, kpos_ref, qpos_ref, dq_ref, dk_ref, dv_ref
):
    rows = q_ref.shape[0]
    scale = DH ** (-0.5)
    allowed = kpos_ref[...] <= qpos_ref[...]
    q, k, v, do = q_ref[...], k_ref[...], v_ref[...], do_ref[...]
    scores = jnp.where(allowed, times_transposed(k, q) * scale, NEG)
    top = jnp.max(scores, axis=0, keepdims=True)
    weights = jnp.exp(scores - top)
    weights = weights * (1.0 / jnp.sum(weights, axis=0, keepdims=True))
    weight_grad = times_transposed(v, do)
    delta = jnp.sum(weights * weight_grad, axis=0, keepdims=True)
    score_grad = (weights * (weight_grad - delta)).astype(bf16)
    dv_ref[...] = matmul(weights.astype(bf16), do).astype(bf16)
    dk = matmul(score_grad, q) * scale
    dk_ref[...] = unspin(dk, cos_ref[...], sin_ref[...]).astype(bf16)
    dq = contract_rows(score_grad, k) * scale
    dq_ref[...] = unspin(dq, cos_ref[:rows], sin_ref[:rows]).astype(bf16)


def attend_back(q, k, v, do, cosine, sine, kpos, qpos):
    rows, length = q.shape[0], k.shape[0]
    once = pl.Buffered(1)
    fixed = lambda a: pl.BlockSpec(a.shape, lambda h: (0, 0), pipeline_mode=once)
    wide = lambda r: pl.BlockSpec((r, DH), lambda h: (0, h))
    shape = lambda r: jax.ShapeDtypeStruct((r, H * DH), bf16)
    return pl.pallas_call(
        attend_back_kernel,
        grid=(H,),
        in_specs=[wide(rows), wide(length), wide(length), wide(rows)]
        + [fixed(cosine), fixed(sine), fixed(kpos), fixed(qpos)],
        out_specs=[wide(rows), wide(length), wide(length)],
        out_shape=[shape(rows), shape(length), shape(length)],
        compiler_params=pltpu.CompilerParams(vmem_limit_bytes=56 << 20),
        cost_estimate=pl.CostEstimate(
            flops=10 * rows * length * H * DH,
            bytes_accessed=2 * 4 * length * H * DH,
            transcendentals=rows * length * H,
        ),
    )(q, k, v, do, cosine, sine, kpos, qpos)


def expert_kernel(x_ref, w_ref, pre_ref, act_ref):
    gate = matmul(x_ref[...], w_ref[:, :EFF])
    up = matmul(x_ref[...], w_ref[:, EFF:])
    pre_ref[:, :EFF] = gate.astype(bf16)
    pre_ref[:, EFF:] = up.astype(bf16)
    act_ref[...] = (gate * jax.nn.sigmoid(gate) * up).astype(bf16)


def expert_forward(x, weight):
    count, width = x.shape
    step = min(512, count)
    rows = lambda n: pl.BlockSpec((step, n), lambda i: (i, 0))
    return pl.pallas_call(
        expert_kernel,
        grid=(count // step,),
        in_specs=[
            rows(width),
            pl.BlockSpec(weight.shape, lambda i: (0, 0), pipeline_mode=pl.Buffered(1)),
        ],
        out_specs=[rows(2 * EFF), rows(EFF)],
        out_shape=[
            jax.ShapeDtypeStruct((count, 2 * EFF), bf16),
            jax.ShapeDtypeStruct((count, EFF), bf16),
        ],
        compiler_params=pltpu.CompilerParams(vmem_limit_bytes=48 << 20),
        cost_estimate=pl.CostEstimate(
            flops=4 * count * width * EFF, bytes_accessed=12 << 20, transcendentals=0
        ),
    )(x, weight)


def expert_back_kernel(grad_ref, w_ref, pre_ref, out_ref):
    act_grad = times_transposed(grad_ref[...], w_ref[...])
    gate = pre_ref[:, :EFF].astype(f32)
    up = pre_ref[:, EFF:].astype(f32)
    sigma = jax.nn.sigmoid(gate)
    out_ref[:, :EFF] = (act_grad * up * (sigma * (1.0 + gate * (1.0 - sigma)))).astype(bf16)
    out_ref[:, EFF:] = (act_grad * (gate * sigma)).astype(bf16)


def expert_back(grad, weight, pre):
    count, width = grad.shape
    step = min(512, count)
    rows = lambda n: pl.BlockSpec((step, n), lambda i: (i, 0))
    return pl.pallas_call(
        expert_back_kernel,
        grid=(count // step,),
        in_specs=[
            rows(width),
            pl.BlockSpec(weight.shape, lambda i: (0, 0), pipeline_mode=pl.Buffered(1)),
            rows(2 * EFF),
        ],
        out_specs=rows(2 * EFF),
        out_shape=jax.ShapeDtypeStruct((count, 2 * EFF), bf16),
        compiler_params=pltpu.CompilerParams(vmem_limit_bytes=48 << 20),
        cost_estimate=pl.CostEstimate(
            flops=2 * count * width * EFF, bytes_accessed=12 << 20, transcendentals=0
        ),
    )(grad, weight, pre)


def widen(x, count):
    groups, rows = count
    x = x.reshape(groups, x.shape[0] // groups, x.shape[1])
    return jnp.pad(x, ((0, 0), (0, rows - x.shape[1]), (0, 0))).reshape(groups * rows, x.shape[2])


def per_device(
    tokens,
    expert_index,
    cotangent,
    gains,
    w_qkv,
    w_attn_out,
    w_router,
    w_shared_in,
    w_shared_out,
    w_expert_in,
    w_expert_out,
):
    rows, width = tokens.shape
    ways, places = lax.axis_size("ep"), lax.axis_size("dp")
    here, place = lax.axis_index("ep"), lax.axis_index("dp")
    experts = w_expert_in.shape[0] * ways
    shard = gains.shape[0]
    down_shard = w_shared_out.shape[0]
    devices = ways * places
    expert_ids = jnp.arange(experts, dtype=jnp.int32)

    local = w_expert_in.shape[0]
    first_low = jnp.concatenate(
        [
            w_qkv.astype(bf16),
            w_router.astype(bf16),
            gains.astype(bf16),
            jnp.zeros((shard, 128 - experts - 2), bf16),
        ],
        axis=1,
    )
    second_low = jnp.concatenate(
        [
            w_attn_out.astype(bf16),
            w_shared_in.astype(bf16),
            widen(w_shared_out.astype(bf16), (1, shard)),
        ],
        axis=1,
    )
    first_line = line_near(first_low)
    expert_in_low, expert_out_low, token_rows, *first_line = after(
        w_expert_in.astype(bf16), w_expert_out.astype(bf16), tokens, *first_line
    )
    token_blocks = earlier_blocks(token_rows)
    expert_weights = [
        (
            lax.all_gather(expert_in_low[e], "dp", axis=0, tiled=True),
            lax.all_gather(expert_out_low[e], "dp", axis=0, tiled=True),
        )
        for e in range(local)
    ]
    first_line = line_end(first_low, first_line)
    second_low, first_line = after(second_low, first_line)
    second_line = line_near(second_low)
    first_near = spread_near(first_line)
    first_far = spread_far(*first_near)
    first_mine = spread_chips(first_line, *first_near, first_far)
    count = len(second_line)
    first_mine, *arrived = after(first_mine, *second_line, *token_blocks)
    second_line, token_blocks = arrived[:count], arrived[count:]
    first_weights = rows_whole(first_mine)
    second_line = line_end(second_low, second_line)
    second_near = spread_near(second_line)
    choose = jnp.sum((expert_index[:, :, None] == expert_ids).astype(f32), axis=1)
    choose_rows = choose.T.astype(bf16)
    choose_near = spread_near(choose_rows)
    choose_mine = spread_chips(choose_rows, *choose_near, spread_far(*choose_near))
    chosen = jnp.concatenate([choose_mine, flip(choose_mine, 1)], axis=0)
    chosen = chosen.transpose(1, 0, 2).reshape(experts, -1).astype(f32)
    up_packed = cotangent

    router_weight = first_weights[:, 3 * width : 3 * width + experts]
    gain_attn = first_weights[:, 3 * width + experts].astype(f32)
    gain_ffn = first_weights[:, 3 * width + experts + 1].astype(f32)

    inputs_all = jnp.concatenate(token_blocks, axis=0).astype(f32)
    inv_first = lax.rsqrt(jnp.mean(inputs_all * inputs_all, axis=-1, keepdims=True) + EPS)
    normed_first = inputs_all * inv_first
    attn_in = (normed_first * gain_attn).astype(bf16)
    inputs = tokens.astype(f32)
    lane = jnp.arange(rows, dtype=jnp.int32)
    steps = jnp.arange(places, dtype=jnp.int32)
    positions = ((place - steps)[:, None] * rows + lane[None, :]).reshape(-1)
    key_pos = jnp.where(positions >= 0, positions, FAR)
    query_pos = place * rows + lane
    frequency = 10000.0 ** (-2.0 * jnp.arange(DH // 2, dtype=f32) / DH)
    angles = positions.astype(f32)[:, None] * frequency[None, :]
    cosine, sine = jnp.cos(angles), jnp.sin(angles)
    cosine = jnp.concatenate([cosine, cosine], axis=1)
    sine = jnp.concatenate([-sine, sine], axis=1)
    attended_low, queries, keys, values = attend(
        attn_in, first_weights, cosine, sine, key_pos[None, :], query_pos[:, None], rows
    )
    *second_near, attended_low = after(*second_near, attended_low)
    second_far = spread_far(*second_near)
    second_weights = rows_whole(spread_chips(second_line, *second_near, second_far))
    attn_weight = second_weights[:, :width]
    shared_in_weight = second_weights[:, width : width + 2 * EFF]
    shared_out_weight = (
        second_weights[:, width + 2 * EFF :]
        .reshape(devices, shard, width)[:, :down_shard]
        .reshape(EFF, width)
    )
    hidden = inputs + matmul(attended_low, attn_weight)
    inv_second = lax.rsqrt(jnp.mean(hidden * hidden, axis=-1, keepdims=True) + EPS)
    normed_second = hidden * inv_second
    ffn_in = (normed_second * gain_ffn).astype(bf16)

    ffn_near = spread_near(ffn_in)

    def route(rows_in):
        logits = matmul(rows_in, router_weight)
        raised = jnp.exp(logits - jnp.max(logits, axis=-1, keepdims=True))
        return raised / jnp.sum(raised, axis=-1, keepdims=True)

    router_probs = route(ffn_in)

    shared_pre = matmul(ffn_in, shared_in_weight)
    *ffn_near, shared_pre = after(*ffn_near, shared_pre)
    ffn_far = spread_far(*ffn_near)
    shared_gate, shared_up = shared_pre[:, :EFF], shared_pre[:, EFF:]
    shared_act = (jax.nn.silu(shared_gate) * shared_up).astype(bf16)
    shared_out = matmul(shared_act, shared_out_weight)
    shared_act_grad = times_transposed(cotangent, shared_out_weight)
    shared_pre_grad = swiglu_back(shared_gate, shared_up, shared_act_grad).astype(bf16)
    *ffn_far, shared_out = after(*ffn_far, shared_out)
    ffn_mine = spread_chips(ffn_in, *ffn_near, ffn_far)
    ffn_other = flip(ffn_mine, 1)
    up_packed, ffn_mine = after(up_packed, ffn_mine)
    up_near = spread_near(up_packed)

    shared_grads = jnp.concatenate(
        [
            contract_rows(ffn_in, shared_pre_grad).astype(bf16),
            widen(contract_rows(shared_act, cotangent).astype(bf16), (devices, shard)),
        ],
        axis=1,
    )
    shared_back = times_transposed(shared_pre_grad, shared_in_weight)
    *up_near, shared_grads = after(*up_near, shared_grads)
    up_far = spread_far(*up_near)
    shared_kept, shared_core = rows_core([shared_grads])

    half = ways // 2 * rows
    ffn_all = jnp.concatenate([ffn_mine, ffn_other], axis=0).reshape(-1, width)
    logits = lax.dot_general(
        router_weight, ffn_all, (((0,), (1,)), ((), ())), preferred_element_type=f32
    )
    raised = jnp.exp(logits - jnp.max(logits, axis=0, keepdims=True))
    all_probs = raised / jnp.sum(raised, axis=0, keepdims=True)

    def reduce_places(grad):
        return lax.psum_scatter(grad.astype(bf16), "dp", scatter_dimension=0, tiled=True).astype(f32)

    out_parts, in_parts, back = [], [], 0.0
    results, gate_rows = [], []
    for e in range(local):
        pre, act = expert_forward(ffn_all, expert_weights[e][0])
        if e == 0:
            *up_far, shared_core, act = after(*up_far, shared_core, act)
            shared_state = rows_near(shared_kept, shared_core)
            up_mine = spread_chips(up_packed, *up_near, up_far)
            upstream_all = jnp.concatenate([up_mine, flip(up_mine, 1)], axis=0)
            upstream_all = upstream_all.reshape(-1, width).astype(f32)
        expert = here * local + e
        gate = jnp.sum(jnp.where(expert_ids[:, None] == expert, all_probs * chosen, 0.0), axis=0)
        gate = gate[:, None]
        result = matmul(act, expert_weights[e][1]).astype(bf16)
        result_wide = result.astype(f32)
        gate_grad = jnp.sum(upstream_all * result_wide, axis=-1).reshape(ways, 1, rows)
        gate_rows.append(jnp.where(expert_ids[:, None] == expert, gate_grad, 0.0))
        results.append((gate, result))
        copy_grad = (gate * upstream_all).astype(bf16)
        if e < local - 1:
            out_grad = contract_rows(act, copy_grad).astype(bf16)
            copy_grad, out_grad = after(copy_grad, out_grad)
            out_parts.append(reduce_places(out_grad))
            pre_grad = expert_back(copy_grad, expert_weights[e][1], pre)
            if e == 0:
                *shared_state, pre_grad = after(*shared_state, pre_grad)
                shared_state = split_far(*shared_state)
            in_grad = contract_rows(ffn_all, pre_grad).astype(bf16)
            pre_grad, in_grad = after(pre_grad, in_grad)
            in_parts.append(reduce_places(in_grad))
            if e == 0:
                *shared_state, in_grad = after(*shared_state, in_grad)
                shared_line = rows_line(*shared_state)
            back = (back + times_transposed(pre_grad, expert_weights[e][0])).astype(bf16)
            back, ffn_all = after(back, ffn_all)
            continue
        sides = (slice(half, 2 * half), slice(0, half))

        def pack(side):
            rows_out = sum(g[side] * r[side].astype(f32) for g, r in results)
            blocks = slice(side.start // rows, side.stop // rows)
            grads_out = sum(g[blocks] for g in gate_rows)
            return jnp.concatenate(
                [
                    rows_out.astype(bf16).reshape(ways // 2, rows, width),
                    jnp.pad(grads_out.astype(bf16), ((0, 0), (0, 0), (0, width - rows))),
                ],
                axis=1,
            )

        def back_of(grad, side):
            total = times_transposed(grad, expert_weights[e][0]) + back[side]
            return total.astype(bf16).reshape(ways // 2, rows, width)

        packs = [pack(side) for side in sides]
        res_core = flip(packs[0], 1)
        copy_grad, packs[1], out_parts[0] = after(copy_grad, packs[1], out_parts[0])
        pre_grad = expert_back(copy_grad, expert_weights[e][1], pre)
        res_core, pre_grad = after(res_core, pre_grad)
        res_state = collect_near(packs[1], res_core)
        back_other = back_of(pre_grad[half:], sides[0])
        back_core = flip(back_other, 1)
        *res_state, pre_grad, back_other = after(*res_state, pre_grad, back_other)
        res_state = split_far(*res_state)
        back_here = back_of(pre_grad[:half], sides[1])
        back_core, back_here, pre_grad, copy_grad, *res_state = after(
            back_core, back_here, pre_grad, copy_grad, *res_state
        )
        back_state = collect_near(back_here, back_core)
        routed = collect_end(*res_state)
        out_grad = contract_rows(act, copy_grad).astype(bf16)
        *back_state, out_grad, pre_grad = after(*back_state, out_grad, pre_grad)
        back_state = split_far(*back_state)
        in_grad = contract_rows(ffn_all, pre_grad).astype(bf16)
        *back_state, in_grad, in_parts[0] = after(*back_state, in_grad, in_parts[0])
        routed_in_grad = collect_end(*back_state)
        out_parts.append(reduce_places(out_grad))
        in_parts.append(reduce_places(in_grad))
    layer_out = (hidden + shared_out + routed[:rows]).astype(bf16)
    prob_grad = routed[rows:, :rows].T * choose
    logit_grad = (
        router_probs * (prob_grad - jnp.sum(router_probs * prob_grad, axis=-1, keepdims=True))
    ).astype(bf16)
    router_grad = contract_rows(ffn_in, logit_grad)

    upstream = cotangent.astype(f32)
    ffn_in_grad = routed_in_grad + times_transposed(logit_grad, router_weight) + shared_back
    gain_ffn_grad = jnp.sum(ffn_in_grad * normed_second, axis=0)
    scaled_second = ffn_in_grad * gain_ffn
    hidden_grad = upstream + inv_second * (
        scaled_second
        - normed_second * jnp.mean(scaled_second * normed_second, axis=-1, keepdims=True)
    )
    branch_grad = hidden_grad.astype(bf16)
    attended_grad = times_transposed(branch_grad, attn_weight).astype(bf16)
    attn_out_grad = contract_rows(attended_low, branch_grad).astype(bf16)
    attn_kept, attn_core = rows_core([attn_out_grad])
    attn_core, attended_grad = after(attn_core, attended_grad)
    attn_state = rows_near(attn_kept, attn_core)
    attended_grad, attn_state[0], out_parts[-1] = after(attended_grad, attn_state[0], out_parts[-1])
    query_grad, key_grad, value_grad = attend_back(
        queries, keys, values, attended_grad, cosine, sine, key_pos[:, None], query_pos[None, :]
    )
    *attn_state, query_grad, key_grad, value_grad = after(
        *attn_state, query_grad, key_grad, value_grad
    )
    attn_state = split_far(*attn_state)
    pair_kept, pair_core = rows_core(
        [
            contract_rows(attn_in, key_grad).astype(bf16),
            contract_rows(attn_in, value_grad).astype(bf16),
        ]
    )
    *attn_state, pair_kept = after(*attn_state, pair_kept)
    attn_line = rows_line(*attn_state)
    attn_in_grads = times_transposed(key_grad, first_weights[:, width : 2 * width]) + times_transposed(
        value_grad, first_weights[:, 2 * width : 3 * width]
    )
    query_back = times_transposed(query_grad, first_weights[:, :width])
    parts = [attn_in_grads[:rows] + query_back] + [
        attn_in_grads[k * rows : (k + 1) * rows] for k in range(1, places)
    ]
    gain_attn_grad = jnp.sum(attn_in_grads * normed_first, axis=0) + jnp.sum(
        query_back * normed_first[:rows], axis=0
    )

    arrived = [
        lax.ppermute(parts[k].astype(bf16), "dp", [(i, i - k) for i in range(k, places)])
        for k in range(1, places)
    ]
    pair_core, gain_attn_grad = after(pair_core, gain_attn_grad)
    pair_state = rows_near(pair_kept, pair_core)
    small_grad = jnp.concatenate(
        [
            router_grad.astype(bf16),
            gain_attn_grad[:, None].astype(bf16),
            gain_ffn_grad[:, None].astype(bf16),
            jnp.zeros((width, 128 - experts - 2), bf16),
        ],
        axis=1,
    )
    query_kept, query_core = rows_core(
        [contract_rows(attn_in[:rows], query_grad).astype(bf16), small_grad]
    )
    query_core, *pair_state = after(query_core, *pair_state)
    query_state = rows_near(query_kept, query_core)
    pair_state = split_far(*pair_state)
    *query_state, pair_state[0], shared_kept, shared_arrived = after(
        *query_state, pair_state[0], *shared_line
    )
    shared_line = rows_last(shared_kept, shared_arrived)
    query_state = split_far(*query_state)
    *pair_state, query_state[0] = after(*pair_state, query_state[0])
    pair_line = rows_line(*pair_state)
    attn_arrived, pair_kept = after(attn_line[1], pair_line[0])
    attn_line, pair_line = (attn_line[0], attn_arrived), (pair_kept, pair_line[1])
    attn_last = rows_last(*attn_line)
    *query_state, _ = after(*query_state, pair_line[0])
    query_line = rows_line(*query_state)
    *arrived, query_kept = after(*arrived, query_line[0])
    query_line = (query_kept, query_line[1])
    attn_in_grad = parts[0] + sum(x.astype(f32) for x in arrived)
    query_line = rows_last(*query_line)
    in_parts[-1], shared_arrived, query_kept = after(in_parts[-1], shared_line[1], query_line[0])
    query_line = (query_kept, query_line[1])
    shared_part = rows_end(shared_line[0], shared_arrived).astype(f32)
    value_key_part = rows_end(*rows_last(*pair_line))
    query_part = rows_end(*query_line)
    attn_out_part = rows_end(*attn_last).astype(f32)
    normed_own, inv_own = normed_first[:rows], inv_first[:rows]
    scaled_first = attn_in_grad * gain_attn
    input_grad = hidden_grad + inv_own * (
        scaled_first - normed_own * jnp.mean(scaled_first * normed_own, axis=-1, keepdims=True)
    )
    expert_in_part = jnp.stack(in_parts, axis=0)
    expert_out_part = jnp.stack(out_parts, axis=0)
    small_part = query_part[:, width:]
    return (
        layer_out,
        input_grad.astype(bf16),
        small_part[:, experts : experts + 2],
        jnp.concatenate(
            [
                query_part[:, :width],
                value_key_part,
            ],
            axis=1,
        ),
        attn_out_part,
        small_part[:, :experts],
        shared_part[:, : 2 * EFF],
        shared_part[:down_shard, 2 * EFF :],
        expert_in_part,
        expert_out_part,
    )


def solution(mesh):
    both = P(("ep", "dp"), None)
    cut = P("ep", "dp", None)
    return jax.shard_map(
        per_device,
        mesh=mesh,
        in_specs=(both,) * 9 + (cut,) * 2,
        out_specs=(both,) * 8 + (cut,) * 2,
        check_vma=False,
    )
```

```python
import functools

import jax
import jax.numpy as jnp
from jax import lax
from jax.experimental import pallas as pl
from jax.experimental.pallas import tpu as pltpu
from jax.sharding import PartitionSpec as P

H = 10
DH = 128
EFF = 896
EPS = 1e-06
NEG = -1e30
FAR = 1 << 30

bf16 = jnp.bfloat16
f32 = jnp.float32


def contract_rows(left_side, right_side):
    return lax.dot_general(
        left_side, right_side, (((0,), (0,)), ((), ())), preferred_element_type=f32
    )


def times_transposed(left_side, right_side):
    return lax.dot_general(
        left_side, right_side, (((1,), (1,)), ((), ())), preferred_element_type=f32
    )


def matmul(left_side, right_side):
    return jnp.dot(left_side, right_side, preferred_element_type=f32)


def swiglu_back(gate_part, up_part, act_grad):
    sigma_gate = jax.nn.sigmoid(gate_part)
    silu_gate = gate_part * sigma_gate
    slope = sigma_gate * (1.0 + gate_part * (1.0 - sigma_gate))
    return jnp.concatenate([act_grad * up_part * slope, act_grad * silu_gate], axis=-1)


def flip(x, bit):
    count = lax.axis_size("ep")
    return lax.ppermute(x, "ep", [(i, i ^ bit) for i in range(count)])


def flip_dp(x, bit):
    count = lax.axis_size("dp")
    return lax.ppermute(x, "dp", [(i, i ^ bit) for i in range(count)])


def add(a, b):
    return a.astype(f32) + b.astype(f32)


def after(*values):
    there = iter(lax.optimization_barrier(tuple(v for v in values if v is not None)))
    return tuple(None if v is None else next(there) for v in values)


def pick(x, index, axis):
    return lax.dynamic_index_in_dim(x, index, axis, keepdims=False)


def put(whole, part, index):
    return lax.dynamic_update_slice(whole, part, (index,) + (0,) * (whole.ndim - 1))


def earlier_blocks(x):
    count = lax.axis_size("dp")
    return [x] + [
        lax.ppermute(x, "dp", [(i, i + step) for i in range(count - step)]) for step in range(1, count)
    ]


def place_bits():
    here, place = lax.axis_index("ep"), lax.axis_index("dp")
    return here & 1, (here >> 1) & 1, (here >> 2) & 1, place & 1, place >> 1


def spread_near(x):
    return [flip(x, 2), flip(x, 4)]


def spread_far(side, down):
    half = side.shape[0] // 2
    return flip(down[:half], 2), flip(side[half:], 4)


def spread_chips(x, side, down, far):
    chip = lax.axis_index("ep") >> 1
    mine = jnp.zeros((4,) + x.shape, x.dtype)
    for k, block in enumerate((x, side, down, jnp.concatenate(far, axis=0))):
        mine = put(mine, block[None], chip ^ k)
    return mine


def line_near(x):
    if lax.axis_size("dp") != 4:
        return [lax.all_gather(x, "dp", axis=0, tiled=False)]
    return [flip_dp(x, bit) for bit in (1, 2, 3)]


def line_end(x, blocks):
    if len(blocks) == 1:
        return blocks[0]
    place = lax.axis_index("dp")
    whole = jnp.zeros((4,) + x.shape, x.dtype)
    for k, block in enumerate([x] + blocks):
        whole = put(whole, block[None], place ^ k)
    return whole


def rows_whole(mine):
    other = flip(mine, 1)
    core = lax.axis_index("ep") & 1
    both = jnp.zeros((4, 2) + mine.shape[1:], mine.dtype)
    both = lax.dynamic_update_slice(both, mine[:, None], (0, core, 0, 0, 0))
    both = lax.dynamic_update_slice(both, other[:, None], (0, 1 - core, 0, 0, 0))
    return both.reshape(-1, mine.shape[-1])


def split_near(one):
    _, side, down, _, _ = place_bits()
    left, right = one[:, :, 0], one[:, :, 1]
    return [
        pick(left, side, 1),
        pick(right, down, 0),
        flip(pick(left, 1 - side, 1), 2),
        flip(pick(right, 1 - down, 0), 4),
    ]


def split_far(left, right, from_side, from_down):
    _, side, down, _, _ = place_bits()
    left = add(left, from_side).astype(bf16)
    right = add(right, from_down).astype(bf16)
    return [
        pick(left, down, 0),
        pick(right, side, 0),
        flip(pick(left, 1 - down, 0), 4),
        flip(pick(right, 1 - side, 0), 2),
    ]


def collect_near(mine, arrived):
    one = add(mine, arrived).astype(bf16)
    return split_near(one.reshape(2, 2, 2, one.shape[1] // 2, one.shape[2]))


def collect_end(left, right, from_down, from_side):
    return jnp.concatenate([add(left, from_down), add(right, from_side)], axis=0)


def rows_core(parts):
    ways, places = lax.axis_size("ep"), lax.axis_size("dp")
    core, _, _, _, _ = place_bits()
    blocks = [
        x.reshape(2, 2, 2, places, x.shape[0] // (ways * places), x.shape[1]) for x in parts
    ]
    half = lambda which: jnp.concatenate([pick(x, which, 2) for x in blocks], axis=-1)
    return half(core), flip(half(1 - core), 1)


def rows_near(kept, arrived):
    one = add(kept, arrived).astype(bf16)
    places = one.shape[2]
    return split_near(one.reshape(one.shape[:2] + (2, places // 2) + one.shape[3:]))


def rows_line(left, right, from_down, from_side):
    left = add(left, from_down).astype(bf16)
    right = add(right, from_side).astype(bf16)
    line = jnp.concatenate([left, right], axis=0)
    _, _, _, odd, _ = place_bits()
    if line.shape[0] != 4:
        rows, width = line.shape[1:]
        total = lax.psum_scatter(
            line.reshape(-1, width), "dp", scatter_dimension=0, tiled=True
        )
        return total, total
    line = line.reshape((2, 2) + line.shape[1:])
    return pick(line, odd, 1), flip_dp(pick(line, 1 - odd, 1), 1)


def rows_last(kept, arrived):
    if kept.ndim == 2:
        return kept.astype(f32), None
    _, _, _, _, upper = place_bits()
    line = add(kept, arrived).astype(bf16)
    return pick(line, upper, 0), flip_dp(pick(line, 1 - upper, 0), 2)


def rows_end(kept, arrived):
    return kept if arrived is None else add(kept, arrived)


def spin(x, cosine, sine):
    return x * cosine + pltpu.roll(x, DH // 2, 1) * sine


def unspin(x, cosine, sine):
    return x * cosine - pltpu.roll(x, DH // 2, 1) * sine


def attend_kernel(
    x_ref, wq_ref, wk_ref, wv_ref, cos_ref, sin_ref, kpos_ref, qpos_ref, o_ref, q_ref, k_ref, v_ref
):
    rows = o_ref.shape[0]
    scale = DH ** (-0.5)
    keys = matmul(x_ref[...], wk_ref[...])
    values = matmul(x_ref[...], wv_ref[...]).astype(bf16)
    queries = matmul(x_ref[:rows], wq_ref[...])
    v_ref[...] = values
    allowed = kpos_ref[...] <= qpos_ref[...]
    for head in range(keys.shape[1] // DH):
        part = slice(head * DH, (head + 1) * DH)
        k = spin(keys[:, part], cos_ref[...], sin_ref[...]).astype(bf16)
        q = spin(queries[:, part], cos_ref[:rows], sin_ref[:rows]).astype(bf16)
        k_ref[:, part] = k
        q_ref[:, part] = q
        scores = jnp.where(allowed, times_transposed(q, k) * scale, NEG)
        top = jnp.max(scores, axis=1, keepdims=True)
        weights = jnp.exp(scores - top)
        total = jnp.sum(weights, axis=1, keepdims=True)
        attended = matmul(weights.astype(bf16), values[:, part]) / total
        o_ref[:, part] = attended.astype(bf16)


def attend(x, weights, cosine, sine, kpos, qpos, rows):
    length, width = x.shape
    cols = 2 * DH
    once = pl.Buffered(1)
    fixed = lambda a: pl.BlockSpec(a.shape, lambda h: (0, 0), pipeline_mode=once)
    wide = lambda r: pl.BlockSpec((r, cols), lambda h: (0, h))
    steps = H * DH // cols
    part = lambda n: pl.BlockSpec((width, cols), lambda h, n=n: (0, h + n * steps))
    shape = lambda r: jax.ShapeDtypeStruct((r, H * DH), bf16)
    return pl.pallas_call(
        attend_kernel,
        grid=(steps,),
        in_specs=[fixed(x), part(0), part(1), part(2)]
        + [fixed(cosine), fixed(sine), fixed(kpos), fixed(qpos)],
        out_specs=[wide(rows), wide(rows), wide(length), wide(length)],
        out_shape=[shape(rows), shape(rows), shape(length), shape(length)],
        compiler_params=pltpu.CompilerParams(vmem_limit_bytes=56 << 20),
        cost_estimate=pl.CostEstimate(
            flops=2 * width * H * DH * (2 * length + rows) + 4 * rows * length * H * DH,
            bytes_accessed=2 * (3 * width * H * DH + 3 * length * width),
            transcendentals=rows * length * H,
        ),
    )(x, weights, weights, weights, cosine, sine, kpos, qpos)


def attend_back_kernel(
    q_ref, k_ref, v_ref, do_ref, cos_ref, sin_ref, kpos_ref, qpos_ref, dq_ref, dk_ref, dv_ref
):
    rows = q_ref.shape[0]
    scale = DH ** (-0.5)
    allowed = kpos_ref[...] <= qpos_ref[...]
    q, k, v, do = q_ref[...], k_ref[...], v_ref[...], do_ref[...]
    scores = jnp.where(allowed, times_transposed(k, q) * scale, NEG)
    top = jnp.max(scores, axis=0, keepdims=True)
    weights = jnp.exp(scores - top)
    weights = weights * (1.0 / jnp.sum(weights, axis=0, keepdims=True))
    weight_grad = times_transposed(v, do)
    delta = jnp.sum(weights * weight_grad, axis=0, keepdims=True)
    score_grad = (weights * (weight_grad - delta)).astype(bf16)
    dv_ref[...] = matmul(weights.astype(bf16), do).astype(bf16)
    dk = matmul(score_grad, q) * scale
    dk_ref[...] = unspin(dk, cos_ref[...], sin_ref[...]).astype(bf16)
    dq = contract_rows(score_grad, k) * scale
    dq_ref[...] = unspin(dq, cos_ref[:rows], sin_ref[:rows]).astype(bf16)


def attend_back(q, k, v, do, cosine, sine, kpos, qpos):
    rows, length = q.shape[0], k.shape[0]
    once = pl.Buffered(1)
    fixed = lambda a: pl.BlockSpec(a.shape, lambda h: (0, 0), pipeline_mode=once)
    wide = lambda r: pl.BlockSpec((r, DH), lambda h: (0, h))
    shape = lambda r: jax.ShapeDtypeStruct((r, H * DH), bf16)
    return pl.pallas_call(
        attend_back_kernel,
        grid=(H,),
        in_specs=[wide(rows), wide(length), wide(length), wide(rows)]
        + [fixed(cosine), fixed(sine), fixed(kpos), fixed(qpos)],
        out_specs=[wide(rows), wide(length), wide(length)],
        out_shape=[shape(rows), shape(length), shape(length)],
        compiler_params=pltpu.CompilerParams(vmem_limit_bytes=56 << 20),
        cost_estimate=pl.CostEstimate(
            flops=10 * rows * length * H * DH,
            bytes_accessed=2 * 4 * length * H * DH,
            transcendentals=rows * length * H,
        ),
    )(q, k, v, do, cosine, sine, kpos, qpos)


def expert_kernel(x_ref, w_ref, pre_ref, act_ref):
    gate = matmul(x_ref[...], w_ref[:, :EFF])
    up = matmul(x_ref[...], w_ref[:, EFF:])
    pre_ref[:, :EFF] = gate.astype(bf16)
    pre_ref[:, EFF:] = up.astype(bf16)
    act_ref[...] = (gate * jax.nn.sigmoid(gate) * up).astype(bf16)


def expert_forward(x, weight):
    count, width = x.shape
    step = min(512, count)
    rows = lambda n: pl.BlockSpec((step, n), lambda i: (i, 0))
    return pl.pallas_call(
        expert_kernel,
        grid=(count // step,),
        in_specs=[
            rows(width),
            pl.BlockSpec(weight.shape, lambda i: (0, 0), pipeline_mode=pl.Buffered(1)),
        ],
        out_specs=[rows(2 * EFF), rows(EFF)],
        out_shape=[
            jax.ShapeDtypeStruct((count, 2 * EFF), bf16),
            jax.ShapeDtypeStruct((count, EFF), bf16),
        ],
        compiler_params=pltpu.CompilerParams(vmem_limit_bytes=48 << 20),
        cost_estimate=pl.CostEstimate(
            flops=4 * count * width * EFF, bytes_accessed=12 << 20, transcendentals=0
        ),
    )(x, weight)


def expert_back_kernel(grad_ref, w_ref, pre_ref, out_ref):
    act_grad = times_transposed(grad_ref[...], w_ref[...])
    gate = pre_ref[:, :EFF].astype(f32)
    up = pre_ref[:, EFF:].astype(f32)
    sigma = jax.nn.sigmoid(gate)
    out_ref[:, :EFF] = (act_grad * up * (sigma * (1.0 + gate * (1.0 - sigma)))).astype(bf16)
    out_ref[:, EFF:] = (act_grad * (gate * sigma)).astype(bf16)


def expert_back(grad, weight, pre):
    count, width = grad.shape
    step = min(512, count)
    rows = lambda n: pl.BlockSpec((step, n), lambda i: (i, 0))
    return pl.pallas_call(
        expert_back_kernel,
        grid=(count // step,),
        in_specs=[
            rows(width),
            pl.BlockSpec(weight.shape, lambda i: (0, 0), pipeline_mode=pl.Buffered(1)),
            rows(2 * EFF),
        ],
        out_specs=rows(2 * EFF),
        out_shape=jax.ShapeDtypeStruct((count, 2 * EFF), bf16),
        compiler_params=pltpu.CompilerParams(vmem_limit_bytes=48 << 20),
        cost_estimate=pl.CostEstimate(
            flops=2 * count * width * EFF, bytes_accessed=12 << 20, transcendentals=0
        ),
    )(grad, weight, pre)


def widen(x, count):
    groups, rows = count
    x = x.reshape(groups, x.shape[0] // groups, x.shape[1])
    return jnp.pad(x, ((0, 0), (0, rows - x.shape[1]), (0, 0))).reshape(groups * rows, x.shape[2])


def per_device(
    tokens,
    expert_index,
    cotangent,
    gains,
    w_qkv,
    w_attn_out,
    w_router,
    w_shared_in,
    w_shared_out,
    w_expert_in,
    w_expert_out,
):
    rows, width = tokens.shape
    ways, places = lax.axis_size("ep"), lax.axis_size("dp")
    here, place = lax.axis_index("ep"), lax.axis_index("dp")
    experts = w_expert_in.shape[0] * ways
    shard = gains.shape[0]
    down_shard = w_shared_out.shape[0]
    devices = ways * places
    expert_ids = jnp.arange(experts, dtype=jnp.int32)

    local = w_expert_in.shape[0]
    first_low = jnp.concatenate(
        [
            w_qkv.astype(bf16),
            w_router.astype(bf16),
            gains.astype(bf16),
            jnp.zeros((shard, 128 - experts - 2), bf16),
        ],
        axis=1,
    )
    second_low = jnp.concatenate(
        [
            w_attn_out.astype(bf16),
            w_shared_in.astype(bf16),
            widen(w_shared_out.astype(bf16), (1, shard)),
        ],
        axis=1,
    )
    first_line = line_near(first_low)
    token_rows, *first_line = after(tokens, *first_line)
    token_blocks = earlier_blocks(token_rows)
    first_line = line_end(first_low, first_line)
    second_low, first_line = after(second_low, first_line)
    second_line = line_near(second_low)
    first_near = spread_near(first_line)
    first_far = spread_far(*first_near)
    first_mine = spread_chips(first_line, *first_near, first_far)
    count = len(second_line)
    first_mine, expert_in_low, expert_out_low, *arrived = after(
        first_mine, w_expert_in.astype(bf16), w_expert_out.astype(bf16), *second_line, *token_blocks
    )
    second_line, token_blocks = arrived[:count], arrived[count:]
    expert_weights = [
        [
            lax.all_gather(expert_in_low[e], "dp", axis=0, tiled=True),
            lax.all_gather(expert_out_low[e], "dp", axis=0, tiled=True),
        ]
        for e in range(local)
    ]
    first_weights = rows_whole(first_mine)
    second_line = line_end(second_low, second_line)
    second_near = spread_near(second_line)
    choose = jnp.sum((expert_index[:, :, None] == expert_ids).astype(f32), axis=1)
    choose_rows = choose.T.astype(bf16)
    choose_near = spread_near(choose_rows)
    choose_mine = spread_chips(choose_rows, *choose_near, spread_far(*choose_near))
    chosen = jnp.concatenate([choose_mine, flip(choose_mine, 1)], axis=0)
    chosen = chosen.transpose(1, 0, 2).reshape(experts, -1).astype(f32)
    up_packed = cotangent

    router_weight = first_weights[:, 3 * width : 3 * width + experts]
    gain_attn = first_weights[:, 3 * width + experts].astype(f32)
    gain_ffn = first_weights[:, 3 * width + experts + 1].astype(f32)

    inputs_all = jnp.concatenate(token_blocks, axis=0).astype(f32)
    inv_first = lax.rsqrt(jnp.mean(inputs_all * inputs_all, axis=-1, keepdims=True) + EPS)
    normed_first = inputs_all * inv_first
    attn_in = (normed_first * gain_attn).astype(bf16)
    inputs = tokens.astype(f32)
    lane = jnp.arange(rows, dtype=jnp.int32)
    steps = jnp.arange(places, dtype=jnp.int32)
    positions = ((place - steps)[:, None] * rows + lane[None, :]).reshape(-1)
    key_pos = jnp.where(positions >= 0, positions, FAR)
    query_pos = place * rows + lane
    frequency = 10000.0 ** (-2.0 * jnp.arange(DH // 2, dtype=f32) / DH)
    angles = positions.astype(f32)[:, None] * frequency[None, :]
    cosine, sine = jnp.cos(angles), jnp.sin(angles)
    cosine = jnp.concatenate([cosine, cosine], axis=1)
    sine = jnp.concatenate([-sine, sine], axis=1)
    attended_low, queries, keys, values = attend(
        attn_in, first_weights, cosine, sine, key_pos[None, :], query_pos[:, None], rows
    )
    *second_near, attended_low = after(*second_near, attended_low)
    second_far = spread_far(*second_near)
    second_weights = rows_whole(spread_chips(second_line, *second_near, second_far))
    attn_weight = second_weights[:, :width]
    shared_in_weight = second_weights[:, width : width + 2 * EFF]
    shared_out_weight = (
        second_weights[:, width + 2 * EFF :]
        .reshape(devices, shard, width)[:, :down_shard]
        .reshape(EFF, width)
    )
    hidden = inputs + matmul(attended_low, attn_weight)
    inv_second = lax.rsqrt(jnp.mean(hidden * hidden, axis=-1, keepdims=True) + EPS)
    normed_second = hidden * inv_second
    ffn_in = (normed_second * gain_ffn).astype(bf16)

    ffn_in, expert_weights[0][0] = after(ffn_in, expert_weights[0][0])
    ffn_near = spread_near(ffn_in)

    def route(rows_in):
        logits = matmul(rows_in, router_weight)
        raised = jnp.exp(logits - jnp.max(logits, axis=-1, keepdims=True))
        return raised / jnp.sum(raised, axis=-1, keepdims=True)

    router_probs = route(ffn_in)

    shared_pre = matmul(ffn_in, shared_in_weight)
    *ffn_near, shared_pre = after(*ffn_near, shared_pre)
    ffn_far = spread_far(*ffn_near)
    shared_gate, shared_up = shared_pre[:, :EFF], shared_pre[:, EFF:]
    shared_act = (jax.nn.silu(shared_gate) * shared_up).astype(bf16)
    shared_out = matmul(shared_act, shared_out_weight)
    shared_act_grad = times_transposed(cotangent, shared_out_weight)
    shared_pre_grad = swiglu_back(shared_gate, shared_up, shared_act_grad).astype(bf16)
    *ffn_far, shared_out = after(*ffn_far, shared_out)
    ffn_mine = spread_chips(ffn_in, *ffn_near, ffn_far)
    ffn_other = flip(ffn_mine, 1)
    up_packed, ffn_mine, expert_weights[0][1] = after(up_packed, ffn_mine, expert_weights[0][1])
    up_near = spread_near(up_packed)

    shared_grads = jnp.concatenate(
        [
            contract_rows(ffn_in, shared_pre_grad).astype(bf16),
            widen(contract_rows(shared_act, cotangent).astype(bf16), (devices, shard)),
        ],
        axis=1,
    )
    shared_back = times_transposed(shared_pre_grad, shared_in_weight)
    *up_near, shared_grads = after(*up_near, shared_grads)
    up_far = spread_far(*up_near)
    shared_kept, shared_core = rows_core([shared_grads])

    half = ways // 2 * rows
    ffn_all = jnp.concatenate([ffn_mine, ffn_other], axis=0).reshape(-1, width)
    logits = lax.dot_general(
        router_weight, ffn_all, (((0,), (1,)), ((), ())), preferred_element_type=f32
    )
    raised = jnp.exp(logits - jnp.max(logits, axis=0, keepdims=True))
    all_probs = raised / jnp.sum(raised, axis=0, keepdims=True)

    def reduce_places(grad):
        return lax.psum_scatter(grad.astype(bf16), "dp", scatter_dimension=0, tiled=True).astype(f32)

    out_parts, in_parts, back = [], [], 0.0
    results, gate_rows = [], []
    for e in range(local):
        pre, act = expert_forward(ffn_all, expert_weights[e][0])
        if e == 0:
            *up_far, shared_core, act = after(*up_far, shared_core, act)
            shared_state = rows_near(shared_kept, shared_core)
            up_mine = spread_chips(up_packed, *up_near, up_far)
            upstream_all = jnp.concatenate([up_mine, flip(up_mine, 1)], axis=0)
            upstream_all = upstream_all.reshape(-1, width).astype(f32)
        expert = here * local + e
        gate = jnp.sum(jnp.where(expert_ids[:, None] == expert, all_probs * chosen, 0.0), axis=0)
        gate = gate[:, None]
        result = matmul(act, expert_weights[e][1]).astype(bf16)
        result_wide = result.astype(f32)
        gate_grad = jnp.sum(upstream_all * result_wide, axis=-1).reshape(ways, 1, rows)
        gate_rows.append(jnp.where(expert_ids[:, None] == expert, gate_grad, 0.0))
        results.append((gate, result))
        copy_grad = (gate * upstream_all).astype(bf16)
        if e < local - 1:
            out_grad = contract_rows(act, copy_grad).astype(bf16)
            copy_grad, out_grad = after(copy_grad, out_grad)
            out_parts.append(reduce_places(out_grad))
            pre_grad = expert_back(copy_grad, expert_weights[e][1], pre)
            if e == 0:
                *shared_state, pre_grad, expert_weights[1][0] = after(
                    *shared_state, pre_grad, expert_weights[1][0]
                )
                shared_state = split_far(*shared_state)
            in_grad = contract_rows(ffn_all, pre_grad).astype(bf16)
            pre_grad, in_grad = after(pre_grad, in_grad)
            in_parts.append(reduce_places(in_grad))
            if e == 0:
                *shared_state, in_grad = after(*shared_state, in_grad)
                shared_line = rows_line(*shared_state)
            back = (back + times_transposed(pre_grad, expert_weights[e][0])).astype(bf16)
            back, ffn_all, expert_weights[e + 1][1] = after(back, ffn_all, expert_weights[e + 1][1])
            continue
        sides = (slice(half, 2 * half), slice(0, half))

        def pack(side):
            rows_out = sum(g[side] * r[side].astype(f32) for g, r in results)
            blocks = slice(side.start // rows, side.stop // rows)
            grads_out = sum(g[blocks] for g in gate_rows)
            return jnp.concatenate(
                [
                    rows_out.astype(bf16).reshape(ways // 2, rows, width),
                    jnp.pad(grads_out.astype(bf16), ((0, 0), (0, 0), (0, width - rows))),
                ],
                axis=1,
            )

        def back_of(grad, side):
            total = times_transposed(grad, expert_weights[e][0]) + back[side]
            return total.astype(bf16).reshape(ways // 2, rows, width)

        packs = [pack(side) for side in sides]
        res_core = flip(packs[0], 1)
        copy_grad, packs[1], out_parts[0] = after(copy_grad, packs[1], out_parts[0])
        pre_grad = expert_back(copy_grad, expert_weights[e][1], pre)
        res_core, pre_grad = after(res_core, pre_grad)
        res_state = collect_near(packs[1], res_core)
        back_other = back_of(pre_grad[half:], sides[0])
        back_core = flip(back_other, 1)
        *res_state, pre_grad, back_other = after(*res_state, pre_grad, back_other)
        res_state = split_far(*res_state)
        back_here = back_of(pre_grad[:half], sides[1])
        back_core, back_here, pre_grad, copy_grad, *res_state = after(
            back_core, back_here, pre_grad, copy_grad, *res_state
        )
        back_state = collect_near(back_here, back_core)
        routed = collect_end(*res_state)
        out_grad = contract_rows(act, copy_grad).astype(bf16)
        *back_state, out_grad, pre_grad = after(*back_state, out_grad, pre_grad)
        back_state = split_far(*back_state)
        in_grad = contract_rows(ffn_all, pre_grad).astype(bf16)
        *back_state, in_grad, in_parts[0] = after(*back_state, in_grad, in_parts[0])
        routed_in_grad = collect_end(*back_state)
        out_parts.append(reduce_places(out_grad))
        in_parts.append(reduce_places(in_grad))
    layer_out = (hidden + shared_out + routed[:rows]).astype(bf16)
    prob_grad = routed[rows:, :rows].T * choose
    logit_grad = (
        router_probs * (prob_grad - jnp.sum(router_probs * prob_grad, axis=-1, keepdims=True))
    ).astype(bf16)
    router_grad = contract_rows(ffn_in, logit_grad)

    upstream = cotangent.astype(f32)
    ffn_in_grad = routed_in_grad + times_transposed(logit_grad, router_weight) + shared_back
    gain_ffn_grad = jnp.sum(ffn_in_grad * normed_second, axis=0)
    scaled_second = ffn_in_grad * gain_ffn
    hidden_grad = upstream + inv_second * (
        scaled_second
        - normed_second * jnp.mean(scaled_second * normed_second, axis=-1, keepdims=True)
    )
    branch_grad = hidden_grad.astype(bf16)
    attended_grad = times_transposed(branch_grad, attn_weight).astype(bf16)
    attn_out_grad = contract_rows(attended_low, branch_grad).astype(bf16)
    attn_kept, attn_core = rows_core([attn_out_grad])
    attn_core, attended_grad = after(attn_core, attended_grad)
    attn_state = rows_near(attn_kept, attn_core)
    attended_grad, attn_state[0] = after(attended_grad, attn_state[0])
    query_grad, key_grad, value_grad = attend_back(
        queries, keys, values, attended_grad, cosine, sine, key_pos[:, None], query_pos[None, :]
    )
    *attn_state, query_grad, key_grad, value_grad = after(
        *attn_state, query_grad, key_grad, value_grad
    )
    attn_state = split_far(*attn_state)
    pair_kept, pair_core = rows_core(
        [
            contract_rows(attn_in, key_grad).astype(bf16),
            contract_rows(attn_in, value_grad).astype(bf16),
        ]
    )
    *attn_state, pair_kept = after(*attn_state, pair_kept)
    attn_line = rows_line(*attn_state)
    attn_in_grads = times_transposed(key_grad, first_weights[:, width : 2 * width]) + times_transposed(
        value_grad, first_weights[:, 2 * width : 3 * width]
    )
    query_back = times_transposed(query_grad, first_weights[:, :width])
    parts = [attn_in_grads[:rows] + query_back] + [
        attn_in_grads[k * rows : (k + 1) * rows] for k in range(1, places)
    ]
    gain_attn_grad = jnp.sum(attn_in_grads * normed_first, axis=0) + jnp.sum(
        query_back * normed_first[:rows], axis=0
    )

    arrived = [
        lax.ppermute(parts[k].astype(bf16), "dp", [(i, i - k) for i in range(k, places)])
        for k in range(1, places)
    ]
    pair_core, gain_attn_grad, out_parts[-1] = after(pair_core, gain_attn_grad, out_parts[-1])
    pair_state = rows_near(pair_kept, pair_core)
    small_grad = jnp.concatenate(
        [
            router_grad.astype(bf16),
            gain_attn_grad[:, None].astype(bf16),
            gain_ffn_grad[:, None].astype(bf16),
            jnp.zeros((width, 128 - experts - 2), bf16),
        ],
        axis=1,
    )
    query_kept, query_core = rows_core(
        [contract_rows(attn_in[:rows], query_grad).astype(bf16), small_grad]
    )
    query_core, *pair_state = after(query_core, *pair_state)
    query_state = rows_near(query_kept, query_core)
    pair_state = split_far(*pair_state)
    *query_state, pair_state[0], shared_kept, shared_arrived = after(
        *query_state, pair_state[0], *shared_line
    )
    shared_line = rows_last(shared_kept, shared_arrived)
    query_state = split_far(*query_state)
    *pair_state, query_state[0] = after(*pair_state, query_state[0])
    pair_line = rows_line(*pair_state)
    attn_arrived, pair_kept = after(attn_line[1], pair_line[0])
    attn_line, pair_line = (attn_line[0], attn_arrived), (pair_kept, pair_line[1])
    attn_last = rows_last(*attn_line)
    *query_state, _ = after(*query_state, pair_line[0])
    query_line = rows_line(*query_state)
    *arrived, query_kept = after(*arrived, query_line[0])
    query_line = (query_kept, query_line[1])
    attn_in_grad = parts[0] + sum(x.astype(f32) for x in arrived)
    query_line = rows_last(*query_line)
    in_parts[-1], shared_arrived, query_kept = after(in_parts[-1], shared_line[1], query_line[0])
    query_line = (query_kept, query_line[1])
    shared_part = rows_end(shared_line[0], shared_arrived).astype(f32)
    value_key_part = rows_end(*rows_last(*pair_line))
    query_part = rows_end(*query_line)
    attn_out_part = rows_end(*attn_last).astype(f32)
    normed_own, inv_own = normed_first[:rows], inv_first[:rows]
    scaled_first = attn_in_grad * gain_attn
    input_grad = hidden_grad + inv_own * (
        scaled_first - normed_own * jnp.mean(scaled_first * normed_own, axis=-1, keepdims=True)
    )
    expert_in_part = jnp.stack(in_parts, axis=0)
    expert_out_part = jnp.stack(out_parts, axis=0)
    small_part = query_part[:, width:]
    return (
        layer_out,
        input_grad.astype(bf16),
        small_part[:, experts : experts + 2],
        jnp.concatenate(
            [
                query_part[:, :width],
                value_key_part,
            ],
            axis=1,
        ),
        attn_out_part,
        small_part[:, :experts],
        shared_part[:, : 2 * EFF],
        shared_part[:down_shard, 2 * EFF :],
        expert_in_part,
        expert_out_part,
    )


def solution(mesh):
    both = P(("ep", "dp"), None)
    cut = P("ep", "dp", None)
    return jax.shard_map(
        per_device,
        mesh=mesh,
        in_specs=(both,) * 9 + (cut,) * 2,
        out_specs=(both,) * 8 + (cut,) * 2,
        check_vma=False,
    )
```

```python
import functools

import jax
import jax.numpy as jnp
from jax import lax
from jax.experimental import pallas as pl
from jax.experimental.pallas import tpu as pltpu
from jax.sharding import PartitionSpec as P

H = 10
DH = 128
EFF = 896
EPS = 1e-06
NEG = -1e30
FAR = 1 << 30

bf16 = jnp.bfloat16
f32 = jnp.float32


def contract_rows(left_side, right_side):
    return lax.dot_general(
        left_side, right_side, (((0,), (0,)), ((), ())), preferred_element_type=f32
    )


def times_transposed(left_side, right_side):
    return lax.dot_general(
        left_side, right_side, (((1,), (1,)), ((), ())), preferred_element_type=f32
    )


def matmul(left_side, right_side):
    return jnp.dot(left_side, right_side, preferred_element_type=f32)


def swiglu_back(gate_part, up_part, act_grad):
    sigma_gate = jax.nn.sigmoid(gate_part)
    silu_gate = gate_part * sigma_gate
    slope = sigma_gate * (1.0 + gate_part * (1.0 - sigma_gate))
    return jnp.concatenate([act_grad * up_part * slope, act_grad * silu_gate], axis=-1)


def flip(x, bit):
    count = lax.axis_size("ep")
    return lax.ppermute(x, "ep", [(i, i ^ bit) for i in range(count)])


def flip_dp(x, bit):
    count = lax.axis_size("dp")
    return lax.ppermute(x, "dp", [(i, i ^ bit) for i in range(count)])


def add(a, b):
    return a.astype(f32) + b.astype(f32)


def after(*values):
    there = iter(lax.optimization_barrier(tuple(v for v in values if v is not None)))
    return tuple(None if v is None else next(there) for v in values)


def pick(x, index, axis):
    return lax.dynamic_index_in_dim(x, index, axis, keepdims=False)


def put(whole, part, index):
    return lax.dynamic_update_slice(whole, part, (index,) + (0,) * (whole.ndim - 1))


def earlier_blocks(x):
    count = lax.axis_size("dp")
    return [x] + [
        lax.ppermute(x, "dp", [(i, i + step) for i in range(count - step)]) for step in range(1, count)
    ]


def place_bits():
    here, place = lax.axis_index("ep"), lax.axis_index("dp")
    return here & 1, (here >> 1) & 1, (here >> 2) & 1, place & 1, place >> 1


def spread_near(x):
    return [flip(x, 2), flip(x, 4)]


def spread_far(side, down):
    half = side.shape[0] // 2
    return flip(down[:half], 2), flip(side[half:], 4)


def spread_chips(x, side, down, far):
    chip = lax.axis_index("ep") >> 1
    mine = jnp.zeros((4,) + x.shape, x.dtype)
    for k, block in enumerate((x, side, down, jnp.concatenate(far, axis=0))):
        mine = put(mine, block[None], chip ^ k)
    return mine


def line_near(x):
    if lax.axis_size("dp") != 4:
        return [lax.all_gather(x, "dp", axis=0, tiled=False)]
    return [flip_dp(x, bit) for bit in (1, 2, 3)]


def line_end(x, blocks):
    if len(blocks) == 1:
        return blocks[0]
    place = lax.axis_index("dp")
    whole = jnp.zeros((4,) + x.shape, x.dtype)
    for k, block in enumerate([x] + blocks):
        whole = put(whole, block[None], place ^ k)
    return whole


def rows_whole(mine):
    other = flip(mine, 1)
    core = lax.axis_index("ep") & 1
    both = jnp.zeros((4, 2) + mine.shape[1:], mine.dtype)
    both = lax.dynamic_update_slice(both, mine[:, None], (0, core, 0, 0, 0))
    both = lax.dynamic_update_slice(both, other[:, None], (0, 1 - core, 0, 0, 0))
    return both.reshape(-1, mine.shape[-1])


def split_near(one):
    _, side, down, _, _ = place_bits()
    left, right = one[:, :, 0], one[:, :, 1]
    return [
        pick(left, side, 1),
        pick(right, down, 0),
        flip(pick(left, 1 - side, 1), 2),
        flip(pick(right, 1 - down, 0), 4),
    ]


def split_far(left, right, from_side, from_down):
    _, side, down, _, _ = place_bits()
    left = add(left, from_side).astype(bf16)
    right = add(right, from_down).astype(bf16)
    return [
        pick(left, down, 0),
        pick(right, side, 0),
        flip(pick(left, 1 - down, 0), 4),
        flip(pick(right, 1 - side, 0), 2),
    ]


def collect_near(mine, arrived):
    one = add(mine, arrived).astype(bf16)
    return split_near(one.reshape(2, 2, 2, one.shape[1] // 2, one.shape[2]))


def collect_end(left, right, from_down, from_side):
    return jnp.concatenate([add(left, from_down), add(right, from_side)], axis=0)


def rows_core(parts):
    ways, places = lax.axis_size("ep"), lax.axis_size("dp")
    core, _, _, _, _ = place_bits()
    blocks = [
        x.reshape(2, 2, 2, places, x.shape[0] // (ways * places), x.shape[1]) for x in parts
    ]
    half = lambda which: jnp.concatenate([pick(x, which, 2) for x in blocks], axis=-1)
    return half(core), flip(half(1 - core), 1)


def rows_near(kept, arrived):
    one = add(kept, arrived).astype(bf16)
    places = one.shape[2]
    return split_near(one.reshape(one.shape[:2] + (2, places // 2) + one.shape[3:]))


def rows_line(left, right, from_down, from_side):
    left = add(left, from_down).astype(bf16)
    right = add(right, from_side).astype(bf16)
    line = jnp.concatenate([left, right], axis=0)
    _, _, _, odd, _ = place_bits()
    if line.shape[0] != 4:
        rows, width = line.shape[1:]
        total = lax.psum_scatter(
            line.reshape(-1, width), "dp", scatter_dimension=0, tiled=True
        )
        return total, total
    line = line.reshape((2, 2) + line.shape[1:])
    return pick(line, odd, 1), flip_dp(pick(line, 1 - odd, 1), 1)


def rows_last(kept, arrived):
    if kept.ndim == 2:
        return kept.astype(f32), None
    _, _, _, _, upper = place_bits()
    line = add(kept, arrived).astype(bf16)
    return pick(line, upper, 0), flip_dp(pick(line, 1 - upper, 0), 2)


def rows_end(kept, arrived):
    return kept if arrived is None else add(kept, arrived)


def spin(x, cosine, sine):
    return x * cosine + pltpu.roll(x, DH // 2, 1) * sine


def unspin(x, cosine, sine):
    return x * cosine - pltpu.roll(x, DH // 2, 1) * sine


def attend_kernel(
    x_ref, wq_ref, wk_ref, wv_ref, cos_ref, sin_ref, kpos_ref, qpos_ref, o_ref, q_ref, k_ref, v_ref
):
    rows = o_ref.shape[0]
    scale = DH ** (-0.5)
    keys = matmul(x_ref[...], wk_ref[...])
    values = matmul(x_ref[...], wv_ref[...]).astype(bf16)
    queries = matmul(x_ref[:rows], wq_ref[...])
    v_ref[...] = values
    allowed = kpos_ref[...] <= qpos_ref[...]
    for head in range(keys.shape[1] // DH):
        part = slice(head * DH, (head + 1) * DH)
        k = spin(keys[:, part], cos_ref[...], sin_ref[...]).astype(bf16)
        q = spin(queries[:, part], cos_ref[:rows], sin_ref[:rows]).astype(bf16)
        k_ref[:, part] = k
        q_ref[:, part] = q
        scores = jnp.where(allowed, times_transposed(q, k) * scale, NEG)
        top = jnp.max(scores, axis=1, keepdims=True)
        weights = jnp.exp(scores - top)
        total = jnp.sum(weights, axis=1, keepdims=True)
        attended = matmul(weights.astype(bf16), values[:, part]) / total
        o_ref[:, part] = attended.astype(bf16)


def attend(x, weights, cosine, sine, kpos, qpos, rows):
    length, width = x.shape
    cols = 2 * DH
    once = pl.Buffered(1)
    fixed = lambda a: pl.BlockSpec(a.shape, lambda h: (0, 0), pipeline_mode=once)
    wide = lambda r: pl.BlockSpec((r, cols), lambda h: (0, h))
    steps = H * DH // cols
    part = lambda n: pl.BlockSpec((width, cols), lambda h, n=n: (0, h + n * steps))
    shape = lambda r: jax.ShapeDtypeStruct((r, H * DH), bf16)
    return pl.pallas_call(
        attend_kernel,
        grid=(steps,),
        in_specs=[fixed(x), part(0), part(1), part(2)]
        + [fixed(cosine), fixed(sine), fixed(kpos), fixed(qpos)],
        out_specs=[wide(rows), wide(rows), wide(length), wide(length)],
        out_shape=[shape(rows), shape(rows), shape(length), shape(length)],
        compiler_params=pltpu.CompilerParams(vmem_limit_bytes=56 << 20),
        cost_estimate=pl.CostEstimate(
            flops=2 * width * H * DH * (2 * length + rows) + 4 * rows * length * H * DH,
            bytes_accessed=2 * (3 * width * H * DH + 3 * length * width),
            transcendentals=rows * length * H,
        ),
    )(x, weights, weights, weights, cosine, sine, kpos, qpos)


def attend_back_kernel(
    q_ref, k_ref, v_ref, do_ref, cos_ref, sin_ref, kpos_ref, qpos_ref, dq_ref, dk_ref, dv_ref
):
    rows = q_ref.shape[0]
    scale = DH ** (-0.5)
    allowed = kpos_ref[...] <= qpos_ref[...]
    q, k, v, do = q_ref[...], k_ref[...], v_ref[...], do_ref[...]
    scores = jnp.where(allowed, times_transposed(k, q) * scale, NEG)
    top = jnp.max(scores, axis=0, keepdims=True)
    weights = jnp.exp(scores - top)
    weights = weights * (1.0 / jnp.sum(weights, axis=0, keepdims=True))
    weight_grad = times_transposed(v, do)
    delta = jnp.sum(weights * weight_grad, axis=0, keepdims=True)
    score_grad = (weights * (weight_grad - delta)).astype(bf16)
    dv_ref[...] = matmul(weights.astype(bf16), do).astype(bf16)
    dk = matmul(score_grad, q) * scale
    dk_ref[...] = unspin(dk, cos_ref[...], sin_ref[...]).astype(bf16)
    dq = contract_rows(score_grad, k) * scale
    dq_ref[...] = unspin(dq, cos_ref[:rows], sin_ref[:rows]).astype(bf16)


def attend_back(q, k, v, do, cosine, sine, kpos, qpos):
    rows, length = q.shape[0], k.shape[0]
    once = pl.Buffered(1)
    fixed = lambda a: pl.BlockSpec(a.shape, lambda h: (0, 0), pipeline_mode=once)
    wide = lambda r: pl.BlockSpec((r, DH), lambda h: (0, h))
    shape = lambda r: jax.ShapeDtypeStruct((r, H * DH), bf16)
    return pl.pallas_call(
        attend_back_kernel,
        grid=(H,),
        in_specs=[wide(rows), wide(length), wide(length), wide(rows)]
        + [fixed(cosine), fixed(sine), fixed(kpos), fixed(qpos)],
        out_specs=[wide(rows), wide(length), wide(length)],
        out_shape=[shape(rows), shape(length), shape(length)],
        compiler_params=pltpu.CompilerParams(vmem_limit_bytes=56 << 20),
        cost_estimate=pl.CostEstimate(
            flops=10 * rows * length * H * DH,
            bytes_accessed=2 * 4 * length * H * DH,
            transcendentals=rows * length * H,
        ),
    )(q, k, v, do, cosine, sine, kpos, qpos)


def expert_kernel(x_ref, w_ref, pre_ref, act_ref):
    gate = matmul(x_ref[...], w_ref[:, :EFF])
    up = matmul(x_ref[...], w_ref[:, EFF:])
    pre_ref[:, :EFF] = gate.astype(bf16)
    pre_ref[:, EFF:] = up.astype(bf16)
    act_ref[...] = (gate * jax.nn.sigmoid(gate) * up).astype(bf16)


def expert_forward(x, weight):
    count, width = x.shape
    step = min(512, count)
    rows = lambda n: pl.BlockSpec((step, n), lambda i: (i, 0))
    return pl.pallas_call(
        expert_kernel,
        grid=(count // step,),
        in_specs=[
            rows(width),
            pl.BlockSpec(weight.shape, lambda i: (0, 0), pipeline_mode=pl.Buffered(1)),
        ],
        out_specs=[rows(2 * EFF), rows(EFF)],
        out_shape=[
            jax.ShapeDtypeStruct((count, 2 * EFF), bf16),
            jax.ShapeDtypeStruct((count, EFF), bf16),
        ],
        compiler_params=pltpu.CompilerParams(vmem_limit_bytes=48 << 20),
        cost_estimate=pl.CostEstimate(
            flops=4 * count * width * EFF, bytes_accessed=12 << 20, transcendentals=0
        ),
    )(x, weight)


def expert_back_kernel(grad_ref, w_ref, pre_ref, out_ref):
    act_grad = times_transposed(grad_ref[...], w_ref[...])
    gate = pre_ref[:, :EFF].astype(f32)
    up = pre_ref[:, EFF:].astype(f32)
    sigma = jax.nn.sigmoid(gate)
    out_ref[:, :EFF] = (act_grad * up * (sigma * (1.0 + gate * (1.0 - sigma)))).astype(bf16)
    out_ref[:, EFF:] = (act_grad * (gate * sigma)).astype(bf16)


def expert_back(grad, weight, pre):
    count, width = grad.shape
    step = min(512, count)
    rows = lambda n: pl.BlockSpec((step, n), lambda i: (i, 0))
    return pl.pallas_call(
        expert_back_kernel,
        grid=(count // step,),
        in_specs=[
            rows(width),
            pl.BlockSpec(weight.shape, lambda i: (0, 0), pipeline_mode=pl.Buffered(1)),
            rows(2 * EFF),
        ],
        out_specs=rows(2 * EFF),
        out_shape=jax.ShapeDtypeStruct((count, 2 * EFF), bf16),
        compiler_params=pltpu.CompilerParams(vmem_limit_bytes=48 << 20),
        cost_estimate=pl.CostEstimate(
            flops=2 * count * width * EFF, bytes_accessed=12 << 20, transcendentals=0
        ),
    )(grad, weight, pre)


def widen(x, count):
    groups, rows = count
    x = x.reshape(groups, x.shape[0] // groups, x.shape[1])
    return jnp.pad(x, ((0, 0), (0, rows - x.shape[1]), (0, 0))).reshape(groups * rows, x.shape[2])


def per_device(
    tokens,
    expert_index,
    cotangent,
    gains,
    w_qkv,
    w_attn_out,
    w_router,
    w_shared_in,
    w_shared_out,
    w_expert_in,
    w_expert_out,
):
    rows, width = tokens.shape
    ways, places = lax.axis_size("ep"), lax.axis_size("dp")
    here, place = lax.axis_index("ep"), lax.axis_index("dp")
    experts = w_expert_in.shape[0] * ways
    shard = gains.shape[0]
    down_shard = w_shared_out.shape[0]
    devices = ways * places
    expert_ids = jnp.arange(experts, dtype=jnp.int32)

    local = w_expert_in.shape[0]
    first_low = jnp.concatenate(
        [
            w_qkv.astype(bf16),
            w_router.astype(bf16),
            gains.astype(bf16),
            jnp.zeros((shard, 128 - experts - 2), bf16),
        ],
        axis=1,
    )
    second_low = jnp.concatenate(
        [
            w_attn_out.astype(bf16),
            w_shared_in.astype(bf16),
            widen(w_shared_out.astype(bf16), (1, shard)),
        ],
        axis=1,
    )
    first_line = line_near(first_low)
    token_rows, *first_line = after(tokens, *first_line)
    token_blocks = earlier_blocks(token_rows)
    first_line = line_end(first_low, first_line)
    second_low, first_line = after(second_low, first_line)
    second_line = line_near(second_low)
    first_near = spread_near(first_line)
    first_far = spread_far(*first_near)
    first_mine = spread_chips(first_line, *first_near, first_far)
    count = len(second_line)
    first_mine, expert_in_low, expert_out_low, *arrived = after(
        first_mine, w_expert_in.astype(bf16), w_expert_out.astype(bf16), *second_line, *token_blocks
    )
    second_line, token_blocks = arrived[:count], arrived[count:]
    expert_weights = [
        [
            lax.all_gather(expert_in_low[e], "dp", axis=0, tiled=True),
            lax.all_gather(expert_out_low[e], "dp", axis=0, tiled=True),
        ]
        for e in range(local)
    ]
    first_weights = rows_whole(first_mine)
    second_line = line_end(second_low, second_line)
    second_near = spread_near(second_line)
    choose = jnp.sum((expert_index[:, :, None] == expert_ids).astype(f32), axis=1)
    choose_rows = choose.T.astype(bf16)
    choose_near = spread_near(choose_rows)
    choose_mine = spread_chips(choose_rows, *choose_near, spread_far(*choose_near))
    chosen = jnp.concatenate([choose_mine, flip(choose_mine, 1)], axis=0)
    chosen = chosen.transpose(1, 0, 2).reshape(experts, -1).astype(f32)
    up_packed = cotangent

    router_weight = first_weights[:, 3 * width : 3 * width + experts]
    gain_attn = first_weights[:, 3 * width + experts].astype(f32)
    gain_ffn = first_weights[:, 3 * width + experts + 1].astype(f32)

    inputs_all = jnp.concatenate(token_blocks, axis=0).astype(f32)
    inv_first = lax.rsqrt(jnp.mean(inputs_all * inputs_all, axis=-1, keepdims=True) + EPS)
    normed_first = inputs_all * inv_first
    attn_in = (normed_first * gain_attn).astype(bf16)
    inputs = tokens.astype(f32)
    lane = jnp.arange(rows, dtype=jnp.int32)
    steps = jnp.arange(places, dtype=jnp.int32)
    positions = ((place - steps)[:, None] * rows + lane[None, :]).reshape(-1)
    key_pos = jnp.where(positions >= 0, positions, FAR)
    query_pos = place * rows + lane
    frequency = 10000.0 ** (-2.0 * jnp.arange(DH // 2, dtype=f32) / DH)
    angles = positions.astype(f32)[:, None] * frequency[None, :]
    cosine, sine = jnp.cos(angles), jnp.sin(angles)
    cosine = jnp.concatenate([cosine, cosine], axis=1)
    sine = jnp.concatenate([-sine, sine], axis=1)
    attended_low, queries, keys, values = attend(
        attn_in, first_weights, cosine, sine, key_pos[None, :], query_pos[:, None], rows
    )
    *second_near, attended_low = after(*second_near, attended_low)
    second_far = spread_far(*second_near)
    second_weights = rows_whole(spread_chips(second_line, *second_near, second_far))
    attn_weight = second_weights[:, :width]
    shared_in_weight = second_weights[:, width : width + 2 * EFF]
    shared_out_weight = (
        second_weights[:, width + 2 * EFF :]
        .reshape(devices, shard, width)[:, :down_shard]
        .reshape(EFF, width)
    )
    hidden = inputs + matmul(attended_low, attn_weight)
    inv_second = lax.rsqrt(jnp.mean(hidden * hidden, axis=-1, keepdims=True) + EPS)
    normed_second = hidden * inv_second
    ffn_in = (normed_second * gain_ffn).astype(bf16)

    ffn_in, expert_weights[0][0] = after(ffn_in, expert_weights[0][0])
    ffn_near = spread_near(ffn_in)

    def route(rows_in):
        logits = matmul(rows_in, router_weight)
        raised = jnp.exp(logits - jnp.max(logits, axis=-1, keepdims=True))
        return raised / jnp.sum(raised, axis=-1, keepdims=True)

    router_probs = route(ffn_in)

    shared_pre = matmul(ffn_in, shared_in_weight)
    *ffn_near, shared_pre = after(*ffn_near, shared_pre)
    ffn_far = spread_far(*ffn_near)
    shared_gate, shared_up = shared_pre[:, :EFF], shared_pre[:, EFF:]
    shared_act = (jax.nn.silu(shared_gate) * shared_up).astype(bf16)
    shared_out = matmul(shared_act, shared_out_weight)
    shared_act_grad = times_transposed(cotangent, shared_out_weight)
    shared_pre_grad = swiglu_back(shared_gate, shared_up, shared_act_grad).astype(bf16)
    *ffn_far, shared_out = after(*ffn_far, shared_out)
    ffn_mine = spread_chips(ffn_in, *ffn_near, ffn_far)
    ffn_other = flip(ffn_mine, 1)
    up_packed, ffn_mine, expert_weights[0][1] = after(up_packed, ffn_mine, expert_weights[0][1])
    up_near = spread_near(up_packed)

    shared_grads = jnp.concatenate(
        [
            contract_rows(ffn_in, shared_pre_grad).astype(bf16),
            widen(contract_rows(shared_act, cotangent).astype(bf16), (devices, shard)),
        ],
        axis=1,
    )
    shared_back = times_transposed(shared_pre_grad, shared_in_weight)
    *up_near, shared_grads = after(*up_near, shared_grads)
    up_far = spread_far(*up_near)
    shared_kept, shared_core = rows_core([shared_grads])

    half = ways // 2 * rows
    ffn_all = jnp.concatenate([ffn_mine, ffn_other], axis=0).reshape(-1, width)
    logits = lax.dot_general(
        router_weight, ffn_all, (((0,), (1,)), ((), ())), preferred_element_type=f32
    )
    raised = jnp.exp(logits - jnp.max(logits, axis=0, keepdims=True))
    all_probs = raised / jnp.sum(raised, axis=0, keepdims=True)

    def reduce_places(grad):
        return lax.psum_scatter(grad.astype(bf16), "dp", scatter_dimension=0, tiled=True).astype(f32)

    out_parts, in_parts, back = [], [], 0.0
    results, gate_rows = [], []
    for e in range(local):
        pre, act = expert_forward(ffn_all, expert_weights[e][0])
        if e:
            act, expert_weights[e][1] = after(act, expert_weights[e][1])
        if e == 0:
            *up_far, shared_core, act = after(*up_far, shared_core, act)
            shared_state = rows_near(shared_kept, shared_core)
            up_mine = spread_chips(up_packed, *up_near, up_far)
            upstream_all = jnp.concatenate([up_mine, flip(up_mine, 1)], axis=0)
            upstream_all = upstream_all.reshape(-1, width).astype(f32)
        expert = here * local + e
        gate = jnp.sum(jnp.where(expert_ids[:, None] == expert, all_probs * chosen, 0.0), axis=0)
        gate = gate[:, None]
        result = matmul(act, expert_weights[e][1]).astype(bf16)
        result_wide = result.astype(f32)
        gate_grad = jnp.sum(upstream_all * result_wide, axis=-1).reshape(ways, 1, rows)
        gate_rows.append(jnp.where(expert_ids[:, None] == expert, gate_grad, 0.0))
        results.append((gate, result))
        copy_grad = (gate * upstream_all).astype(bf16)
        if e < local - 1:
            out_grad = contract_rows(act, copy_grad).astype(bf16)
            copy_grad, out_grad = after(copy_grad, out_grad)
            out_parts.append(reduce_places(out_grad))
            pre_grad = expert_back(copy_grad, expert_weights[e][1], pre)
            if e == 0:
                *shared_state, pre_grad, expert_weights[1][0] = after(
                    *shared_state, pre_grad, expert_weights[1][0]
                )
                shared_state = split_far(*shared_state)
            in_grad = contract_rows(ffn_all, pre_grad).astype(bf16)
            pre_grad, in_grad = after(pre_grad, in_grad)
            in_parts.append(reduce_places(in_grad))
            if e == 0:
                *shared_state, in_grad = after(*shared_state, in_grad)
                shared_line = rows_line(*shared_state)
            back = (back + times_transposed(pre_grad, expert_weights[e][0])).astype(bf16)
            back, ffn_all = after(back, ffn_all)
            continue
        sides = (slice(half, 2 * half), slice(0, half))

        def pack(side):
            rows_out = sum(g[side] * r[side].astype(f32) for g, r in results)
            blocks = slice(side.start // rows, side.stop // rows)
            grads_out = sum(g[blocks] for g in gate_rows)
            return jnp.concatenate(
                [
                    rows_out.astype(bf16).reshape(ways // 2, rows, width),
                    jnp.pad(grads_out.astype(bf16), ((0, 0), (0, 0), (0, width - rows))),
                ],
                axis=1,
            )

        def back_of(grad, side):
            total = times_transposed(grad, expert_weights[e][0]) + back[side]
            return total.astype(bf16).reshape(ways // 2, rows, width)

        packs = [pack(side) for side in sides]
        res_core = flip(packs[0], 1)
        copy_grad, packs[1], out_parts[0] = after(copy_grad, packs[1], out_parts[0])
        pre_grad = expert_back(copy_grad, expert_weights[e][1], pre)
        res_core, pre_grad = after(res_core, pre_grad)
        res_state = collect_near(packs[1], res_core)
        back_other = back_of(pre_grad[half:], sides[0])
        back_core = flip(back_other, 1)
        *res_state, pre_grad, back_other = after(*res_state, pre_grad, back_other)
        res_state = split_far(*res_state)
        back_here = back_of(pre_grad[:half], sides[1])
        back_core, back_here, pre_grad, copy_grad, *res_state = after(
            back_core, back_here, pre_grad, copy_grad, *res_state
        )
        back_state = collect_near(back_here, back_core)
        routed = collect_end(*res_state)
        out_grad = contract_rows(act, copy_grad).astype(bf16)
        *back_state, out_grad, pre_grad = after(*back_state, out_grad, pre_grad)
        back_state = split_far(*back_state)
        in_grad = contract_rows(ffn_all, pre_grad).astype(bf16)
        *back_state, in_grad, in_parts[0] = after(*back_state, in_grad, in_parts[0])
        routed_in_grad = collect_end(*back_state)
        out_parts.append(reduce_places(out_grad))
        in_parts.append(reduce_places(in_grad))
    layer_out = (hidden + shared_out + routed[:rows]).astype(bf16)
    prob_grad = routed[rows:, :rows].T * choose
    logit_grad = (
        router_probs * (prob_grad - jnp.sum(router_probs * prob_grad, axis=-1, keepdims=True))
    ).astype(bf16)
    router_grad = contract_rows(ffn_in, logit_grad)

    upstream = cotangent.astype(f32)
    ffn_in_grad = routed_in_grad + times_transposed(logit_grad, router_weight) + shared_back
    gain_ffn_grad = jnp.sum(ffn_in_grad * normed_second, axis=0)
    scaled_second = ffn_in_grad * gain_ffn
    hidden_grad = upstream + inv_second * (
        scaled_second
        - normed_second * jnp.mean(scaled_second * normed_second, axis=-1, keepdims=True)
    )
    branch_grad = hidden_grad.astype(bf16)
    attended_grad = times_transposed(branch_grad, attn_weight).astype(bf16)
    attn_out_grad = contract_rows(attended_low, branch_grad).astype(bf16)
    attn_kept, attn_core = rows_core([attn_out_grad])
    attn_core, attended_grad = after(attn_core, attended_grad)
    attn_state = rows_near(attn_kept, attn_core)
    attended_grad, attn_state[0] = after(attended_grad, attn_state[0])
    query_grad, key_grad, value_grad = attend_back(
        queries, keys, values, attended_grad, cosine, sine, key_pos[:, None], query_pos[None, :]
    )
    *attn_state, query_grad, key_grad, value_grad = after(
        *attn_state, query_grad, key_grad, value_grad
    )
    attn_state = split_far(*attn_state)
    pair_kept, pair_core = rows_core(
        [
            contract_rows(attn_in, key_grad).astype(bf16),
            contract_rows(attn_in, value_grad).astype(bf16),
        ]
    )
    *attn_state, pair_kept = after(*attn_state, pair_kept)
    attn_line = rows_line(*attn_state)
    attn_in_grads = times_transposed(key_grad, first_weights[:, width : 2 * width]) + times_transposed(
        value_grad, first_weights[:, 2 * width : 3 * width]
    )
    query_back = times_transposed(query_grad, first_weights[:, :width])
    parts = [attn_in_grads[:rows] + query_back] + [
        attn_in_grads[k * rows : (k + 1) * rows] for k in range(1, places)
    ]
    gain_attn_grad = jnp.sum(attn_in_grads * normed_first, axis=0) + jnp.sum(
        query_back * normed_first[:rows], axis=0
    )

    arrived = [
        lax.ppermute(parts[k].astype(bf16), "dp", [(i, i - k) for i in range(k, places)])
        for k in range(1, places)
    ]
    pair_core, gain_attn_grad, out_parts[-1] = after(pair_core, gain_attn_grad, out_parts[-1])
    pair_state = rows_near(pair_kept, pair_core)
    small_grad = jnp.concatenate(
        [
            router_grad.astype(bf16),
            gain_attn_grad[:, None].astype(bf16),
            gain_ffn_grad[:, None].astype(bf16),
            jnp.zeros((width, 128 - experts - 2), bf16),
        ],
        axis=1,
    )
    query_kept, query_core = rows_core(
        [contract_rows(attn_in[:rows], query_grad).astype(bf16), small_grad]
    )
    query_core, *pair_state = after(query_core, *pair_state)
    query_state = rows_near(query_kept, query_core)
    pair_state = split_far(*pair_state)
    *query_state, pair_state[0], shared_kept, shared_arrived = after(
        *query_state, pair_state[0], *shared_line
    )
    shared_line = rows_last(shared_kept, shared_arrived)
    query_state = split_far(*query_state)
    *pair_state, query_state[0] = after(*pair_state, query_state[0])
    pair_line = rows_line(*pair_state)
    *query_state, _ = after(*query_state, pair_line[0])
    query_line = rows_line(*query_state)
    *arrived, query_kept = after(*arrived, query_line[0])
    query_line = (query_kept, query_line[1])
    attn_in_grad = parts[0] + sum(x.astype(f32) for x in arrived)
    query_line = rows_last(*query_line)
    attn_arrived, query_kept = after(attn_line[1], query_line[0])
    query_line = (query_kept, query_line[1])
    attn_last = rows_last(attn_line[0], attn_arrived)
    in_parts[-1], shared_arrived, query_kept = after(in_parts[-1], shared_line[1], query_line[0])
    query_line = (query_kept, query_line[1])
    shared_part = rows_end(shared_line[0], shared_arrived).astype(f32)
    value_key_part = rows_end(*rows_last(*pair_line))
    query_part = rows_end(*query_line)
    attn_out_part = rows_end(*attn_last).astype(f32)
    normed_own, inv_own = normed_first[:rows], inv_first[:rows]
    scaled_first = attn_in_grad * gain_attn
    input_grad = hidden_grad + inv_own * (
        scaled_first - normed_own * jnp.mean(scaled_first * normed_own, axis=-1, keepdims=True)
    )
    expert_in_part = jnp.stack(in_parts, axis=0)
    expert_out_part = jnp.stack(out_parts, axis=0)
    small_part = query_part[:, width:]
    return (
        layer_out,
        input_grad.astype(bf16),
        small_part[:, experts : experts + 2],
        jnp.concatenate(
            [
                query_part[:, :width],
                value_key_part,
            ],
            axis=1,
        ),
        attn_out_part,
        small_part[:, :experts],
        shared_part[:, : 2 * EFF],
        shared_part[:down_shard, 2 * EFF :],
        expert_in_part,
        expert_out_part,
    )


def solution(mesh):
    both = P(("ep", "dp"), None)
    cut = P("ep", "dp", None)
    return jax.shard_map(
        per_device,
        mesh=mesh,
        in_specs=(both,) * 9 + (cut,) * 2,
        out_specs=(both,) * 8 + (cut,) * 2,
        check_vma=False,
    )
```

```python
import functools

import jax
import jax.numpy as jnp
from jax import lax
from jax.experimental import pallas as pl
from jax.experimental.pallas import tpu as pltpu
from jax.sharding import PartitionSpec as P

H = 10
DH = 128
EFF = 896
EPS = 1e-06
NEG = -1e30
FAR = 1 << 30

bf16 = jnp.bfloat16
f32 = jnp.float32


def contract_rows(left_side, right_side):
    return lax.dot_general(
        left_side, right_side, (((0,), (0,)), ((), ())), preferred_element_type=f32
    )


def times_transposed(left_side, right_side):
    return lax.dot_general(
        left_side, right_side, (((1,), (1,)), ((), ())), preferred_element_type=f32
    )


def matmul(left_side, right_side):
    return jnp.dot(left_side, right_side, preferred_element_type=f32)


def swiglu_back(gate_part, up_part, act_grad):
    sigma_gate = jax.nn.sigmoid(gate_part)
    silu_gate = gate_part * sigma_gate
    slope = sigma_gate * (1.0 + gate_part * (1.0 - sigma_gate))
    return jnp.concatenate([act_grad * up_part * slope, act_grad * silu_gate], axis=-1)


def flip(x, bit):
    count = lax.axis_size("ep")
    return lax.ppermute(x, "ep", [(i, i ^ bit) for i in range(count)])


def flip_dp(x, bit):
    count = lax.axis_size("dp")
    return lax.ppermute(x, "dp", [(i, i ^ bit) for i in range(count)])


def add(a, b):
    return a.astype(f32) + b.astype(f32)


def after(*values):
    there = iter(lax.optimization_barrier(tuple(v for v in values if v is not None)))
    return tuple(None if v is None else next(there) for v in values)


def pick(x, index, axis):
    return lax.dynamic_index_in_dim(x, index, axis, keepdims=False)


def put(whole, part, index):
    return lax.dynamic_update_slice(whole, part, (index,) + (0,) * (whole.ndim - 1))


def earlier_blocks(x):
    count = lax.axis_size("dp")
    return [x] + [
        lax.ppermute(x, "dp", [(i, i + step) for i in range(count - step)]) for step in range(1, count)
    ]


def place_bits():
    here, place = lax.axis_index("ep"), lax.axis_index("dp")
    return here & 1, (here >> 1) & 1, (here >> 2) & 1, place & 1, place >> 1


def spread_near(x):
    return [flip(x, 2), flip(x, 4)]


def spread_far(side, down):
    half = side.shape[0] // 2
    return flip(down[:half], 2), flip(side[half:], 4)


def spread_chips(x, side, down, far):
    chip = lax.axis_index("ep") >> 1
    mine = jnp.zeros((4,) + x.shape, x.dtype)
    for k, block in enumerate((x, side, down, jnp.concatenate(far, axis=0))):
        mine = put(mine, block[None], chip ^ k)
    return mine


def line_near(x):
    if lax.axis_size("dp") != 4:
        return [lax.all_gather(x, "dp", axis=0, tiled=False)]
    return [flip_dp(x, bit) for bit in (1, 2, 3)]


def line_end(x, blocks):
    if len(blocks) == 1:
        return blocks[0]
    place = lax.axis_index("dp")
    whole = jnp.zeros((4,) + x.shape, x.dtype)
    for k, block in enumerate([x] + blocks):
        whole = put(whole, block[None], place ^ k)
    return whole


def rows_whole(mine):
    other = flip(mine, 1)
    core = lax.axis_index("ep") & 1
    both = jnp.zeros((4, 2) + mine.shape[1:], mine.dtype)
    both = lax.dynamic_update_slice(both, mine[:, None], (0, core, 0, 0, 0))
    both = lax.dynamic_update_slice(both, other[:, None], (0, 1 - core, 0, 0, 0))
    return both.reshape(-1, mine.shape[-1])


def split_near(one):
    _, side, down, _, _ = place_bits()
    left, right = one[:, :, 0], one[:, :, 1]
    return [
        pick(left, side, 1),
        pick(right, down, 0),
        flip(pick(left, 1 - side, 1), 2),
        flip(pick(right, 1 - down, 0), 4),
    ]


def split_far(left, right, from_side, from_down):
    _, side, down, _, _ = place_bits()
    left = add(left, from_side).astype(bf16)
    right = add(right, from_down).astype(bf16)
    return [
        pick(left, down, 0),
        pick(right, side, 0),
        flip(pick(left, 1 - down, 0), 4),
        flip(pick(right, 1 - side, 0), 2),
    ]


def collect_near(mine, arrived):
    one = add(mine, arrived).astype(bf16)
    return split_near(one.reshape(2, 2, 2, one.shape[1] // 2, one.shape[2]))


def collect_end(left, right, from_down, from_side):
    return jnp.concatenate([add(left, from_down), add(right, from_side)], axis=0)


def rows_core(parts):
    ways, places = lax.axis_size("ep"), lax.axis_size("dp")
    core, _, _, _, _ = place_bits()
    blocks = [
        x.reshape(2, 2, 2, places, x.shape[0] // (ways * places), x.shape[1]) for x in parts
    ]
    half = lambda which: jnp.concatenate([pick(x, which, 2) for x in blocks], axis=-1)
    return half(core), flip(half(1 - core), 1)


def rows_near(kept, arrived):
    one = add(kept, arrived).astype(bf16)
    places = one.shape[2]
    return split_near(one.reshape(one.shape[:2] + (2, places // 2) + one.shape[3:]))


def rows_line(left, right, from_down, from_side):
    left = add(left, from_down).astype(bf16)
    right = add(right, from_side).astype(bf16)
    line = jnp.concatenate([left, right], axis=0)
    _, _, _, odd, _ = place_bits()
    if line.shape[0] != 4:
        rows, width = line.shape[1:]
        total = lax.psum_scatter(
            line.reshape(-1, width), "dp", scatter_dimension=0, tiled=True
        )
        return total, total
    line = line.reshape((2, 2) + line.shape[1:])
    return pick(line, odd, 1), flip_dp(pick(line, 1 - odd, 1), 1)


def rows_last(kept, arrived):
    if kept.ndim == 2:
        return kept.astype(f32), None
    _, _, _, _, upper = place_bits()
    line = add(kept, arrived).astype(bf16)
    return pick(line, upper, 0), flip_dp(pick(line, 1 - upper, 0), 2)


def rows_end(kept, arrived):
    return kept if arrived is None else add(kept, arrived)


def spin(x, cosine, sine):
    return x * cosine + pltpu.roll(x, DH // 2, 1) * sine


def unspin(x, cosine, sine):
    return x * cosine - pltpu.roll(x, DH // 2, 1) * sine


def attend_kernel(
    x_ref, wq_ref, wk_ref, wv_ref, cos_ref, sin_ref, kpos_ref, qpos_ref, o_ref, q_ref, k_ref, v_ref
):
    rows = o_ref.shape[0]
    scale = DH ** (-0.5)
    keys = matmul(x_ref[...], wk_ref[...])
    values = matmul(x_ref[...], wv_ref[...]).astype(bf16)
    queries = matmul(x_ref[:rows], wq_ref[...])
    v_ref[...] = values
    allowed = kpos_ref[...] <= qpos_ref[...]
    for head in range(keys.shape[1] // DH):
        part = slice(head * DH, (head + 1) * DH)
        k = spin(keys[:, part], cos_ref[...], sin_ref[...]).astype(bf16)
        q = spin(queries[:, part], cos_ref[:rows], sin_ref[:rows]).astype(bf16)
        k_ref[:, part] = k
        q_ref[:, part] = q
        scores = jnp.where(allowed, times_transposed(q, k) * scale, NEG)
        top = jnp.max(scores, axis=1, keepdims=True)
        weights = jnp.exp(scores - top)
        total = jnp.sum(weights, axis=1, keepdims=True)
        attended = matmul(weights.astype(bf16), values[:, part]) / total
        o_ref[:, part] = attended.astype(bf16)


def attend(x, weights, cosine, sine, kpos, qpos, rows):
    length, width = x.shape
    cols = 2 * DH
    once = pl.Buffered(1)
    fixed = lambda a: pl.BlockSpec(a.shape, lambda h: (0, 0), pipeline_mode=once)
    wide = lambda r: pl.BlockSpec((r, cols), lambda h: (0, h))
    steps = H * DH // cols
    part = lambda n: pl.BlockSpec((width, cols), lambda h, n=n: (0, h + n * steps))
    shape = lambda r: jax.ShapeDtypeStruct((r, H * DH), bf16)
    return pl.pallas_call(
        attend_kernel,
        grid=(steps,),
        in_specs=[fixed(x), part(0), part(1), part(2)]
        + [fixed(cosine), fixed(sine), fixed(kpos), fixed(qpos)],
        out_specs=[wide(rows), wide(rows), wide(length), wide(length)],
        out_shape=[shape(rows), shape(rows), shape(length), shape(length)],
        compiler_params=pltpu.CompilerParams(vmem_limit_bytes=56 << 20),
        cost_estimate=pl.CostEstimate(
            flops=2 * width * H * DH * (2 * length + rows) + 4 * rows * length * H * DH,
            bytes_accessed=2 * (3 * width * H * DH + 3 * length * width),
            transcendentals=rows * length * H,
        ),
    )(x, weights, weights, weights, cosine, sine, kpos, qpos)


def attend_back_kernel(
    q_ref, k_ref, v_ref, do_ref, cos_ref, sin_ref, kpos_ref, qpos_ref, dq_ref, dk_ref, dv_ref
):
    rows = q_ref.shape[0]
    scale = DH ** (-0.5)
    allowed = kpos_ref[...] <= qpos_ref[...]
    q, k, v, do = q_ref[...], k_ref[...], v_ref[...], do_ref[...]
    scores = jnp.where(allowed, times_transposed(k, q) * scale, NEG)
    top = jnp.max(scores, axis=0, keepdims=True)
    weights = jnp.exp(scores - top)
    weights = weights * (1.0 / jnp.sum(weights, axis=0, keepdims=True))
    weight_grad = times_transposed(v, do)
    delta = jnp.sum(weights * weight_grad, axis=0, keepdims=True)
    score_grad = (weights * (weight_grad - delta)).astype(bf16)
    dv_ref[...] = matmul(weights.astype(bf16), do).astype(bf16)
    dk = matmul(score_grad, q) * scale
    dk_ref[...] = unspin(dk, cos_ref[...], sin_ref[...]).astype(bf16)
    dq = contract_rows(score_grad, k) * scale
    dq_ref[...] = unspin(dq, cos_ref[:rows], sin_ref[:rows]).astype(bf16)


def attend_back(q, k, v, do, cosine, sine, kpos, qpos):
    rows, length = q.shape[0], k.shape[0]
    once = pl.Buffered(1)
    fixed = lambda a: pl.BlockSpec(a.shape, lambda h: (0, 0), pipeline_mode=once)
    wide = lambda r: pl.BlockSpec((r, DH), lambda h: (0, h))
    shape = lambda r: jax.ShapeDtypeStruct((r, H * DH), bf16)
    return pl.pallas_call(
        attend_back_kernel,
        grid=(H,),
        in_specs=[wide(rows), wide(length), wide(length), wide(rows)]
        + [fixed(cosine), fixed(sine), fixed(kpos), fixed(qpos)],
        out_specs=[wide(rows), wide(length), wide(length)],
        out_shape=[shape(rows), shape(length), shape(length)],
        compiler_params=pltpu.CompilerParams(vmem_limit_bytes=56 << 20),
        cost_estimate=pl.CostEstimate(
            flops=10 * rows * length * H * DH,
            bytes_accessed=2 * 4 * length * H * DH,
            transcendentals=rows * length * H,
        ),
    )(q, k, v, do, cosine, sine, kpos, qpos)


def expert_kernel(x_ref, w_ref, pre_ref, act_ref):
    gate = matmul(x_ref[...], w_ref[:, :EFF])
    up = matmul(x_ref[...], w_ref[:, EFF:])
    pre_ref[:, :EFF] = gate.astype(bf16)
    pre_ref[:, EFF:] = up.astype(bf16)
    act_ref[...] = (gate * jax.nn.sigmoid(gate) * up).astype(bf16)


def expert_forward(x, weight):
    count, width = x.shape
    step = min(512, count)
    rows = lambda n: pl.BlockSpec((step, n), lambda i: (i, 0))
    return pl.pallas_call(
        expert_kernel,
        grid=(count // step,),
        in_specs=[
            rows(width),
            pl.BlockSpec(weight.shape, lambda i: (0, 0), pipeline_mode=pl.Buffered(1)),
        ],
        out_specs=[rows(2 * EFF), rows(EFF)],
        out_shape=[
            jax.ShapeDtypeStruct((count, 2 * EFF), bf16),
            jax.ShapeDtypeStruct((count, EFF), bf16),
        ],
        compiler_params=pltpu.CompilerParams(vmem_limit_bytes=48 << 20),
        cost_estimate=pl.CostEstimate(
            flops=4 * count * width * EFF, bytes_accessed=12 << 20, transcendentals=0
        ),
    )(x, weight)


def expert_back_kernel(grad_ref, w_ref, pre_ref, out_ref):
    act_grad = times_transposed(grad_ref[...], w_ref[...])
    gate = pre_ref[:, :EFF].astype(f32)
    up = pre_ref[:, EFF:].astype(f32)
    sigma = jax.nn.sigmoid(gate)
    out_ref[:, :EFF] = (act_grad * up * (sigma * (1.0 + gate * (1.0 - sigma)))).astype(bf16)
    out_ref[:, EFF:] = (act_grad * (gate * sigma)).astype(bf16)


def expert_back(grad, weight, pre):
    count, width = grad.shape
    step = min(512, count)
    rows = lambda n: pl.BlockSpec((step, n), lambda i: (i, 0))
    return pl.pallas_call(
        expert_back_kernel,
        grid=(count // step,),
        in_specs=[
            rows(width),
            pl.BlockSpec(weight.shape, lambda i: (0, 0), pipeline_mode=pl.Buffered(1)),
            rows(2 * EFF),
        ],
        out_specs=rows(2 * EFF),
        out_shape=jax.ShapeDtypeStruct((count, 2 * EFF), bf16),
        compiler_params=pltpu.CompilerParams(vmem_limit_bytes=48 << 20),
        cost_estimate=pl.CostEstimate(
            flops=2 * count * width * EFF, bytes_accessed=12 << 20, transcendentals=0
        ),
    )(grad, weight, pre)


def widen(x, count):
    groups, rows = count
    x = x.reshape(groups, x.shape[0] // groups, x.shape[1])
    return jnp.pad(x, ((0, 0), (0, rows - x.shape[1]), (0, 0))).reshape(groups * rows, x.shape[2])


def per_device(
    tokens,
    expert_index,
    cotangent,
    gains,
    w_qkv,
    w_attn_out,
    w_router,
    w_shared_in,
    w_shared_out,
    w_expert_in,
    w_expert_out,
):
    rows, width = tokens.shape
    ways, places = lax.axis_size("ep"), lax.axis_size("dp")
    here, place = lax.axis_index("ep"), lax.axis_index("dp")
    experts = w_expert_in.shape[0] * ways
    shard = gains.shape[0]
    down_shard = w_shared_out.shape[0]
    devices = ways * places
    expert_ids = jnp.arange(experts, dtype=jnp.int32)

    local = w_expert_in.shape[0]
    first_low = jnp.concatenate(
        [
            w_qkv.astype(bf16),
            w_router.astype(bf16),
            gains.astype(bf16),
            jnp.zeros((shard, 128 - experts - 2), bf16),
        ],
        axis=1,
    )
    second_low = jnp.concatenate(
        [
            w_attn_out.astype(bf16),
            w_shared_in.astype(bf16),
            widen(w_shared_out.astype(bf16), (1, shard)),
        ],
        axis=1,
    )
    first_line = line_near(first_low)
    token_rows, *first_line = after(tokens, *first_line)
    token_blocks = earlier_blocks(token_rows)
    first_line = line_end(first_low, first_line)
    second_low, first_line = after(second_low, first_line)
    second_line = line_near(second_low)
    first_near = spread_near(first_line)
    first_far = spread_far(*first_near)
    first_mine = spread_chips(first_line, *first_near, first_far)
    count = len(second_line)
    first_mine, expert_in_low, expert_out_low, *arrived = after(
        first_mine, w_expert_in.astype(bf16), w_expert_out.astype(bf16), *second_line, *token_blocks
    )
    second_line, token_blocks = arrived[:count], arrived[count:]
    expert_weights = [
        [
            lax.all_gather(expert_in_low[e], "dp", axis=0, tiled=True),
            lax.all_gather(expert_out_low[e], "dp", axis=0, tiled=True),
        ]
        for e in range(local)
    ]
    first_weights = rows_whole(first_mine)
    second_line = line_end(second_low, second_line)
    second_near = spread_near(second_line)
    choose = jnp.sum((expert_index[:, :, None] == expert_ids).astype(f32), axis=1)
    choose_rows = choose.T.astype(bf16)
    choose_near = spread_near(choose_rows)
    choose_mine = spread_chips(choose_rows, *choose_near, spread_far(*choose_near))
    chosen = jnp.concatenate([choose_mine, flip(choose_mine, 1)], axis=0)
    chosen = chosen.transpose(1, 0, 2).reshape(experts, -1).astype(f32)
    up_packed = cotangent

    router_weight = first_weights[:, 3 * width : 3 * width + experts]
    gain_attn = first_weights[:, 3 * width + experts].astype(f32)
    gain_ffn = first_weights[:, 3 * width + experts + 1].astype(f32)

    inputs_all = jnp.concatenate(token_blocks, axis=0).astype(f32)
    inv_first = lax.rsqrt(jnp.mean(inputs_all * inputs_all, axis=-1, keepdims=True) + EPS)
    normed_first = inputs_all * inv_first
    attn_in = (normed_first * gain_attn).astype(bf16)
    inputs = tokens.astype(f32)
    lane = jnp.arange(rows, dtype=jnp.int32)
    steps = jnp.arange(places, dtype=jnp.int32)
    positions = ((place - steps)[:, None] * rows + lane[None, :]).reshape(-1)
    key_pos = jnp.where(positions >= 0, positions, FAR)
    query_pos = place * rows + lane
    frequency = 10000.0 ** (-2.0 * jnp.arange(DH // 2, dtype=f32) / DH)
    angles = positions.astype(f32)[:, None] * frequency[None, :]
    cosine, sine = jnp.cos(angles), jnp.sin(angles)
    cosine = jnp.concatenate([cosine, cosine], axis=1)
    sine = jnp.concatenate([-sine, sine], axis=1)
    attended_low, queries, keys, values = attend(
        attn_in, first_weights, cosine, sine, key_pos[None, :], query_pos[:, None], rows
    )
    *second_near, attended_low = after(*second_near, attended_low)
    second_far = spread_far(*second_near)
    second_weights = rows_whole(spread_chips(second_line, *second_near, second_far))
    attn_weight = second_weights[:, :width]
    shared_in_weight = second_weights[:, width : width + 2 * EFF]
    shared_out_weight = (
        second_weights[:, width + 2 * EFF :]
        .reshape(devices, shard, width)[:, :down_shard]
        .reshape(EFF, width)
    )
    hidden = inputs + matmul(attended_low, attn_weight)
    inv_second = lax.rsqrt(jnp.mean(hidden * hidden, axis=-1, keepdims=True) + EPS)
    normed_second = hidden * inv_second
    ffn_in = (normed_second * gain_ffn).astype(bf16)

    ffn_in, expert_weights[0][0] = after(ffn_in, expert_weights[0][0])
    ffn_near = spread_near(ffn_in)

    def route(rows_in):
        logits = matmul(rows_in, router_weight)
        raised = jnp.exp(logits - jnp.max(logits, axis=-1, keepdims=True))
        return raised / jnp.sum(raised, axis=-1, keepdims=True)

    router_probs = route(ffn_in)

    shared_pre = matmul(ffn_in, shared_in_weight)
    *ffn_near, shared_pre = after(*ffn_near, shared_pre)
    ffn_far = spread_far(*ffn_near)
    shared_gate, shared_up = shared_pre[:, :EFF], shared_pre[:, EFF:]
    shared_act = (jax.nn.silu(shared_gate) * shared_up).astype(bf16)
    shared_out = matmul(shared_act, shared_out_weight)
    shared_act_grad = times_transposed(cotangent, shared_out_weight)
    shared_pre_grad = swiglu_back(shared_gate, shared_up, shared_act_grad).astype(bf16)
    *ffn_far, shared_out = after(*ffn_far, shared_out)
    ffn_mine = spread_chips(ffn_in, *ffn_near, ffn_far)
    ffn_other = flip(ffn_mine, 1)
    up_packed, ffn_mine, expert_weights[0][1] = after(up_packed, ffn_mine, expert_weights[0][1])
    up_near = spread_near(up_packed)

    shared_grads = jnp.concatenate(
        [
            contract_rows(ffn_in, shared_pre_grad).astype(bf16),
            widen(contract_rows(shared_act, cotangent).astype(bf16), (devices, shard)),
        ],
        axis=1,
    )
    shared_back = times_transposed(shared_pre_grad, shared_in_weight)
    *up_near, shared_grads = after(*up_near, shared_grads)
    up_far = spread_far(*up_near)
    shared_kept, shared_core = rows_core([shared_grads])

    half = ways // 2 * rows
    ffn_all = jnp.concatenate([ffn_mine, ffn_other], axis=0).reshape(-1, width)
    logits = lax.dot_general(
        router_weight, ffn_all, (((0,), (1,)), ((), ())), preferred_element_type=f32
    )
    raised = jnp.exp(logits - jnp.max(logits, axis=0, keepdims=True))
    all_probs = raised / jnp.sum(raised, axis=0, keepdims=True)

    def reduce_places(grad):
        return lax.psum_scatter(grad.astype(bf16), "dp", scatter_dimension=0, tiled=True).astype(f32)

    out_parts, in_parts, back = [], [], 0.0
    results, gate_rows = [], []
    for e in range(local):
        pre, act = expert_forward(ffn_all, expert_weights[e][0])
        if e:
            act, expert_weights[e][1] = after(act, expert_weights[e][1])
        if e == 0:
            *up_far, shared_core, act = after(*up_far, shared_core, act)
            shared_state = rows_near(shared_kept, shared_core)
            up_mine = spread_chips(up_packed, *up_near, up_far)
            upstream_all = jnp.concatenate([up_mine, flip(up_mine, 1)], axis=0)
            upstream_all = upstream_all.reshape(-1, width).astype(f32)
        expert = here * local + e
        gate = jnp.sum(jnp.where(expert_ids[:, None] == expert, all_probs * chosen, 0.0), axis=0)
        gate = gate[:, None]
        result = matmul(act, expert_weights[e][1]).astype(bf16)
        result_wide = result.astype(f32)
        gate_grad = jnp.sum(upstream_all * result_wide, axis=-1).reshape(ways, 1, rows)
        gate_rows.append(jnp.where(expert_ids[:, None] == expert, gate_grad, 0.0))
        results.append((gate, result))
        copy_grad = (gate * upstream_all).astype(bf16)
        if e < local - 1:
            out_grad = contract_rows(act, copy_grad).astype(bf16)
            copy_grad, out_grad = after(copy_grad, out_grad)
            out_parts.append(reduce_places(out_grad))
            pre_grad = expert_back(copy_grad, expert_weights[e][1], pre)
            if e == 0:
                *shared_state, pre_grad, expert_weights[1][0] = after(
                    *shared_state, pre_grad, expert_weights[1][0]
                )
                shared_state = split_far(*shared_state)
            in_grad = contract_rows(ffn_all, pre_grad).astype(bf16)
            pre_grad, in_grad = after(pre_grad, in_grad)
            in_parts.append(reduce_places(in_grad))
            if e == 0:
                *shared_state, in_grad = after(*shared_state, in_grad)
                shared_line = rows_line(*shared_state)
            back = (back + times_transposed(pre_grad, expert_weights[e][0])).astype(bf16)
            back, ffn_all = after(back, ffn_all)
            continue
        sides = (slice(half, 2 * half), slice(0, half))

        def pack(side):
            rows_out = sum(g[side] * r[side].astype(f32) for g, r in results)
            blocks = slice(side.start // rows, side.stop // rows)
            grads_out = sum(g[blocks] for g in gate_rows)
            return jnp.concatenate(
                [
                    rows_out.astype(bf16).reshape(ways // 2, rows, width),
                    jnp.pad(grads_out.astype(bf16), ((0, 0), (0, 0), (0, width - rows))),
                ],
                axis=1,
            )

        def back_of(grad, side):
            total = times_transposed(grad, expert_weights[e][0]) + back[side]
            return total.astype(bf16).reshape(ways // 2, rows, width)

        packs = [pack(side) for side in sides]
        res_core = flip(packs[0], 1)
        copy_grad, packs[1], out_parts[0] = after(copy_grad, packs[1], out_parts[0])
        pre_grad = expert_back(copy_grad, expert_weights[e][1], pre)
        res_core, pre_grad = after(res_core, pre_grad)
        res_state = collect_near(packs[1], res_core)
        back_other = back_of(pre_grad[half:], sides[0])
        back_core = flip(back_other, 1)
        *res_state, pre_grad, back_other = after(*res_state, pre_grad, back_other)
        res_state = split_far(*res_state)
        back_here = back_of(pre_grad[:half], sides[1])
        back_core, back_here, pre_grad, copy_grad, *res_state = after(
            back_core, back_here, pre_grad, copy_grad, *res_state
        )
        back_state = collect_near(back_here, back_core)
        routed = collect_end(*res_state)
        out_grad = contract_rows(act, copy_grad).astype(bf16)
        *back_state, out_grad, pre_grad = after(*back_state, out_grad, pre_grad)
        back_state = split_far(*back_state)
        in_grad = contract_rows(ffn_all, pre_grad).astype(bf16)
        *back_state, in_grad, in_parts[0] = after(*back_state, in_grad, in_parts[0])
        routed_in_grad = collect_end(*back_state)
        out_parts.append(reduce_places(out_grad))
        in_parts.append(reduce_places(in_grad))
    layer_out = (hidden + shared_out + routed[:rows]).astype(bf16)
    prob_grad = routed[rows:, :rows].T * choose
    logit_grad = (
        router_probs * (prob_grad - jnp.sum(router_probs * prob_grad, axis=-1, keepdims=True))
    ).astype(bf16)
    router_grad = contract_rows(ffn_in, logit_grad)

    upstream = cotangent.astype(f32)
    ffn_in_grad = routed_in_grad + times_transposed(logit_grad, router_weight) + shared_back
    gain_ffn_grad = jnp.sum(ffn_in_grad * normed_second, axis=0)
    scaled_second = ffn_in_grad * gain_ffn
    hidden_grad = upstream + inv_second * (
        scaled_second
        - normed_second * jnp.mean(scaled_second * normed_second, axis=-1, keepdims=True)
    )
    branch_grad = hidden_grad.astype(bf16)
    attended_grad = times_transposed(branch_grad, attn_weight).astype(bf16)
    attn_out_grad = contract_rows(attended_low, branch_grad).astype(bf16)
    attn_kept, attn_core = rows_core([attn_out_grad])
    attn_core, attended_grad = after(attn_core, attended_grad)
    attn_state = rows_near(attn_kept, attn_core)
    attended_grad, attn_state[0] = after(attended_grad, attn_state[0])
    query_grad, key_grad, value_grad = attend_back(
        queries, keys, values, attended_grad, cosine, sine, key_pos[:, None], query_pos[None, :]
    )
    *attn_state, query_grad, key_grad, value_grad, out_parts[-1] = after(
        *attn_state, query_grad, key_grad, value_grad, out_parts[-1]
    )
    attn_state = split_far(*attn_state)
    pair_kept, pair_core = rows_core(
        [
            contract_rows(attn_in, key_grad).astype(bf16),
            contract_rows(attn_in, value_grad).astype(bf16),
        ]
    )
    *attn_state, pair_kept = after(*attn_state, pair_kept)
    attn_line = rows_line(*attn_state)
    attn_in_grads = times_transposed(key_grad, first_weights[:, width : 2 * width]) + times_transposed(
        value_grad, first_weights[:, 2 * width : 3 * width]
    )
    query_back = times_transposed(query_grad, first_weights[:, :width])
    parts = [attn_in_grads[:rows] + query_back] + [
        attn_in_grads[k * rows : (k + 1) * rows] for k in range(1, places)
    ]
    gain_attn_grad = jnp.sum(attn_in_grads * normed_first, axis=0) + jnp.sum(
        query_back * normed_first[:rows], axis=0
    )

    arrived = [
        lax.ppermute(parts[k].astype(bf16), "dp", [(i, i - k) for i in range(k, places)])
        for k in range(1, places)
    ]
    pair_core, gain_attn_grad = after(pair_core, gain_attn_grad)
    pair_state = rows_near(pair_kept, pair_core)
    small_grad = jnp.concatenate(
        [
            router_grad.astype(bf16),
            gain_attn_grad[:, None].astype(bf16),
            gain_ffn_grad[:, None].astype(bf16),
            jnp.zeros((width, 128 - experts - 2), bf16),
        ],
        axis=1,
    )
    query_kept, query_core = rows_core(
        [contract_rows(attn_in[:rows], query_grad).astype(bf16), small_grad]
    )
    query_core, *pair_state = after(query_core, *pair_state)
    query_state = rows_near(query_kept, query_core)
    pair_state = split_far(*pair_state)
    *query_state, pair_state[0], shared_kept, shared_arrived = after(
        *query_state, pair_state[0], *shared_line
    )
    shared_line = rows_last(shared_kept, shared_arrived)
    query_state = split_far(*query_state)
    *pair_state, query_state[0] = after(*pair_state, query_state[0])
    pair_line = rows_line(*pair_state)
    *query_state, _ = after(*query_state, pair_line[0])
    query_line = rows_line(*query_state)
    *arrived, query_kept = after(*arrived, query_line[0])
    query_line = (query_kept, query_line[1])
    attn_in_grad = parts[0] + sum(x.astype(f32) for x in arrived)
    query_line = rows_last(*query_line)
    attn_arrived, query_kept = after(attn_line[1], query_line[0])
    query_line = (query_kept, query_line[1])
    attn_last = rows_last(attn_line[0], attn_arrived)
    in_parts[-1], shared_arrived, query_kept = after(in_parts[-1], shared_line[1], query_line[0])
    query_line = (query_kept, query_line[1])
    shared_part = rows_end(shared_line[0], shared_arrived).astype(f32)
    value_key_part = rows_end(*rows_last(*pair_line))
    query_part = rows_end(*query_line)
    attn_out_part = rows_end(*attn_last).astype(f32)
    normed_own, inv_own = normed_first[:rows], inv_first[:rows]
    scaled_first = attn_in_grad * gain_attn
    input_grad = hidden_grad + inv_own * (
        scaled_first - normed_own * jnp.mean(scaled_first * normed_own, axis=-1, keepdims=True)
    )
    expert_in_part = jnp.stack(in_parts, axis=0)
    expert_out_part = jnp.stack(out_parts, axis=0)
    small_part = query_part[:, width:]
    return (
        layer_out,
        input_grad.astype(bf16),
        small_part[:, experts : experts + 2],
        jnp.concatenate(
            [
                query_part[:, :width],
                value_key_part,
            ],
            axis=1,
        ),
        attn_out_part,
        small_part[:, :experts],
        shared_part[:, : 2 * EFF],
        shared_part[:down_shard, 2 * EFF :],
        expert_in_part,
        expert_out_part,
    )


def solution(mesh):
    both = P(("ep", "dp"), None)
    cut = P("ep", "dp", None)
    return jax.shard_map(
        per_device,
        mesh=mesh,
        in_specs=(both,) * 9 + (cut,) * 2,
        out_specs=(both,) * 8 + (cut,) * 2,
        check_vma=False,
    )
```
